32 devices in a mesh: by: 4 (over z), bx: 8 (over y, x, core).
Axes of the slice: x: 2, y: 2, z: 4, core: 2. Of those that a mesh axis runs over, the one named last changes fastest.
Arguments:
- tracers: float32 [20, 128, 16, 2048], P(None, ('by', 'bx')), may hold values from 0 to 1
- vertical_speed: float32 [20, 128, 2048], P(None, ('by', 'bx')), may hold values from -0.4 to 0.4
- diffusivity: float32 [20, 128, 2048], P(None, ('by', 'bx')), may hold values from 0.02 to 2
- buoyancy_force: bfloat16 [20, 128, 2048], P(None, ('by', 'bx')), may hold values from -2.1 to 2.1
- wet_levels: int32 [128, 2048], P(('by', 'bx')), may hold values from 0 to 20
- surface_patch: int32 [128, 2048], P(('by', 'bx')), may hold values from 0 to 15
- prior_height: float32 [128, 2048], P(('by', 'bx')), may hold values from -5 to 5
- land_mask: int32 [128, 16, 128], P(('by', 'bx')), may hold values 0 or 1
- baroclinic_map: int32 [128], replicated, may hold values from 0 to 127, as said below
- barotropic_map: int32 [128], replicated, may hold values from 0 to 127, as said below
Outputs:
- new_tracers: float32 [20, 128, 16, 2048], P(None, ('by', 'bx'))
- surface_height: float32 [128, 16, 128], P(('by', 'bx'))
The draws below stay inside these ranges and needn't reach their ends.
Inputs may be any that keep to these rules, and one draw needn't show every extreme that they name: baroclinic_map[s] is the geographic block held in baroclinic slot s, blocks numbered row by row with 32 to a block row; it lies in block row s // 32, and every block appears once. barotropic_map[s] is the geographic block held in barotropic slot s, blocks numbered row by row with 32 to a block row; it lies in block row s // 32, and every block appears once.
All inputs are finite; a program needn't handle non-finite values. No bound on the sum of `land_mask` on one device may be relied on, other than what follows from the above.
Results may differ from the reference program's by a relative error of at most 0.0003.
Values sent between devices are 32-bit elements; how exact they have to be, the bound alone decides.
No kernel may reach another device: no remote copies, remote signals or barrier semaphores. Data moves between devices by JAX's collectives and lax.ppermute only.
A program may use at most 128 MiB of HBM per device.

```python
import math
import jax
import jax.numpy as jnp
from jax import lax

BH = 16
BW = 128
LEV = 20
TR = 16
ITERS = 6
GBX = 32
NB = 128
CELLS = 2048
N_BY = 4


def band_permutation(key):
    band_count = NB // GBX
    scores = jax.random.randint(key, (band_count, GBX), 0, 1 << 20) * GBX + jnp.arange(GBX, dtype=jnp.int32)[None, :]
    ordering = jnp.argsort(scores, axis=1, stable=True).astype(jnp.int32)
    offsets = (jnp.arange(band_count, dtype=jnp.int32) * GBX)[:, None]
    return (ordering + offsets).reshape(NB).astype(jnp.int32)


def draw_baroclinic_map(key, part):
    return band_permutation(jax.random.fold_in(key, 11))


def draw_barotropic_map(key, part):
    return band_permutation(jax.random.fold_in(key, 23))


def slot_offsets(key, reach):
    return jax.random.uniform(key, (NB,), jnp.float32, -reach, reach)


def draw_prior_height(key, part):
    offsets = slot_offsets(jax.random.fold_in(key, 31), 3.0)
    base = jnp.clip(0.5 * jax.random.normal(jax.random.fold_in(key, 33), (NB, CELLS), jnp.float32), -2.0, 2.0)
    return (base + offsets[:, None]).astype(jnp.float32)


def draw_buoyancy_force(key, part):
    offsets = slot_offsets(jax.random.fold_in(key, 41), 0.3)
    base = jnp.clip(0.3 * jax.random.normal(jax.random.fold_in(key, 43), (LEV, NB, CELLS), jnp.float32), -1.8, 1.8)
    level_index = lax.broadcasted_iota(jnp.int32, (LEV, 1, 1), 0)
    top_level = (level_index == 0).astype(jnp.float32)
    return (base + top_level * offsets[None, :, None]).astype(jnp.bfloat16)


def plant(drawn, rng, least, high):
    extent = drawn.shape
    index_at = [jax.random.randint(jax.random.fold_in(rng, axis), (), 0, extent[axis]) for axis in range(len(extent))]
    drawn = drawn.at[tuple(index_at)].set(least)
    longest = extent.index(max(extent))
    index_at[longest] = (index_at[longest] + 1) % extent[longest]
    return drawn.at[tuple(index_at)].set(high)


def shard_levels(rng, dims, cuts, least, high):
    def one(position, shards_of):
        steps = jax.random.uniform(jax.random.fold_in(jax.random.fold_in(rng, 6), position), (shards_of,), jnp.float32, least / len(cuts), high / len(cuts))
        return jnp.repeat(jnp.exp(steps), dims[position] // shards_of).reshape((-1,) + (1,) * (len(dims) - position - 1))

    level = one(*cuts[0])
    for cut in cuts[1:]:
        level = level * one(*cut)
    return level


def setup_inputs(seed: int = 0) -> dict:
    key_list = jax.random.split(jax.random.key(seed), 11)
    return {
        "tracers": jnp.clip(1.0 * jax.random.uniform(key_list[0], (LEV, NB, TR, CELLS), jnp.float32) ** shard_levels(key_list[0], (LEV, NB, TR, CELLS), ((1, 32),), -0.2, 0.2), 0.0, 1.0),
        "vertical_speed": jnp.clip(jax.random.uniform(key_list[1], (LEV, NB, CELLS), jnp.float32, -0.4, 0.4) * shard_levels(key_list[1], (LEV, NB, CELLS), ((1, 32),), -0.4, 0.0), -0.4, 0.4),
        "diffusivity": jnp.clip(jnp.exp(math.log(2.0) - 4.6051702 * jax.random.uniform(key_list[2], (LEV, NB, CELLS), jnp.float32) ** shard_levels(key_list[2], (LEV, NB, CELLS), ((1, 32),), -0.2, 0.2)), 0.02, 2.0),
        "buoyancy_force": draw_buoyancy_force(jax.random.fold_in(key_list[10], 71), 0),
        "wet_levels": plant(jax.random.randint(key_list[4], (NB, CELLS), 0, LEV + 1), jax.random.fold_in(key_list[4], 1), 0, LEV).astype(jnp.int32),
        "surface_patch": plant(jax.random.randint(key_list[5], (NB, CELLS), 0, TR), jax.random.fold_in(key_list[5], 1), 0, TR - 1).astype(jnp.int32),
        "prior_height": draw_prior_height(jax.random.fold_in(key_list[10], 71), 0),
        "land_mask": plant((jax.random.randint(key_list[7], (NB, BH, BW), 0, 8) < 7).astype(jnp.int32), jax.random.fold_in(key_list[7], 1), 0, 1),
        "baroclinic_map": draw_baroclinic_map(jax.random.fold_in(key_list[10], 71), 0),
        "barotropic_map": draw_barotropic_map(jax.random.fold_in(key_list[10], 71), 0),
    }


RESTORE = 0.5
SURFACE = 0.1
FACE_SCALE = 2.0


def column_step(tracers, vertical_speed, diffusivity, wet_levels, surface_patch):
    depth_index = lax.broadcasted_iota(jnp.int32, vertical_speed.shape, 0)
    wet_level = (depth_index < wet_levels[None]).astype(jnp.float32)
    open_faces = (depth_index + 1 < wet_levels[None]).astype(jnp.float32)
    speed_open = (vertical_speed * open_faces)[:, :, None]
    shifted_up = jnp.concatenate([tracers[1:], jnp.zeros_like(tracers[:1])], axis=0)
    flux_below = jnp.maximum(speed_open, 0.0) * shifted_up + jnp.minimum(speed_open, 0.0) * tracers
    flux_above = jnp.concatenate([jnp.zeros_like(flux_below[:1]), flux_below[:-1]], axis=0)
    advected = wet_level[:, :, None] * (tracers + flux_below - flux_above)
    mixing = diffusivity * open_faces
    mixing_above = jnp.concatenate([jnp.zeros_like(mixing[:1]), mixing[:-1]], axis=0)
    surface_row = (depth_index == 0).astype(jnp.float32) * wet_level * RESTORE
    diagonal = 1.0 + mixing + mixing_above + surface_row
    tracer_ids = lax.broadcasted_iota(jnp.int32, (1, tracers.shape[2], 1), 1)
    targets = (surface_patch[:, None, :] == tracer_ids).astype(jnp.float32)
    right_side = advected + surface_row[:, :, None] * targets[None]

    def forward(carry, layer):
        ratio_prev, value_prev = carry
        lower_band, diag_now, upper_band, right_now = layer
        pivot_now = diag_now - lower_band * ratio_prev
        ratio_now = upper_band / pivot_now
        value_now = (right_now - lower_band[:, None] * value_prev) / pivot_now[:, None]
        return (ratio_now, value_now), (ratio_now, value_now)

    start_carry = (jnp.zeros(mixing.shape[1:], jnp.float32), jnp.zeros(tracers.shape[1:], jnp.float32))
    ignored, (ratios, values) = lax.scan(forward, start_carry, (-mixing_above, diagonal, -mixing, right_side))

    def backward(following, layer):
        ratio_now, value_now = layer
        solved_now = value_now - ratio_now[:, None] * following
        return solved_now, solved_now

    ignored_too, solved = lax.scan(backward, jnp.zeros(tracers.shape[1:], jnp.float32), (ratios, values), reverse=True)
    return solved


def to_grid(blocks_flat, block_map):
    shaped = blocks_flat.reshape(NB, BH, BW)
    ordered = jnp.zeros_like(shaped).at[block_map].set(shaped)
    return ordered.reshape(N_BY, GBX, BH, BW).transpose(0, 2, 1, 3).reshape(N_BY * BH, GBX * BW)


def from_grid(grid, block_map):
    ordered = grid.reshape(N_BY, BH, GBX, BW).transpose(0, 2, 1, 3).reshape(NB, BH, BW)
    return ordered[block_map]


def next_rows(grid):
    return jnp.concatenate([grid[1:], jnp.zeros_like(grid[:1])], axis=0)


def prev_rows(grid):
    return jnp.concatenate([jnp.zeros_like(grid[:1]), grid[:-1]], axis=0)


def reference(tracers, vertical_speed, diffusivity, buoyancy_force, wet_levels, surface_patch, prior_height, land_mask, baroclinic_map, barotropic_map):
    def one_slot(column_items):
        slot_tracers, slot_speed, slot_mixing, slot_wet, slot_patch = column_items
        stepped = column_step(slot_tracers[:, None], slot_speed[:, None], slot_mixing[:, None], slot_wet[None], slot_patch[None])
        return stepped[:, 0]

    stepped_all = lax.map(one_slot, (jnp.moveaxis(tracers, 1, 0), jnp.moveaxis(vertical_speed, 1, 0), jnp.moveaxis(diffusivity, 1, 0), wet_levels, surface_patch))
    new_tracers = jnp.moveaxis(stepped_all, 0, 1)

    depth_index = lax.broadcasted_iota(jnp.int32, buoyancy_force.shape, 0)
    wet_level = (depth_index < wet_levels[None]).astype(jnp.float32)
    forcing = jnp.sum(wet_level * buoyancy_force.astype(jnp.float32), axis=0)
    forcing_grid = to_grid(forcing, baroclinic_map)
    depth_grid = to_grid(wet_levels.astype(jnp.float32), baroclinic_map)
    prior_grid = to_grid(prior_height, baroclinic_map)
    ocean_grid = to_grid(land_mask.astype(jnp.float32), barotropic_map)

    face_factor = FACE_SCALE / LEV
    east_face = face_factor * jnp.minimum(depth_grid, jnp.roll(depth_grid, -1, axis=1)) * ocean_grid * jnp.roll(ocean_grid, -1, axis=1)
    west_face = jnp.roll(east_face, 1, axis=1)
    south_face = face_factor * jnp.minimum(depth_grid, next_rows(depth_grid)) * ocean_grid * next_rows(ocean_grid)
    north_face = prev_rows(south_face)
    centre_weight = SURFACE * ocean_grid + (1.0 - ocean_grid)
    precond_diagonal = centre_weight + east_face + west_face + south_face + north_face

    def operate(field_grid):
        centre = centre_weight * field_grid
        result = centre + east_face * (field_grid - jnp.roll(field_grid, -1, axis=1))
        result = result + west_face * (field_grid - jnp.roll(field_grid, 1, axis=1))
        result = result + south_face * (field_grid - next_rows(field_grid))
        return result + north_face * (field_grid - prev_rows(field_grid))

    solution = ocean_grid * prior_grid
    residual = ocean_grid * forcing_grid - operate(solution)
    precond = residual / precond_diagonal
    direction = precond
    norm_now = jnp.sum(residual * precond)
    for step_index in range(ITERS):
        image_field = operate(direction)
        step_size = norm_now / jnp.sum(direction * image_field)
        solution = solution + step_size * direction
        residual = residual - step_size * image_field
        precond = residual / precond_diagonal
        norm_next = jnp.sum(residual * precond)
        direction = precond + (norm_next / norm_now) * direction
        norm_now = norm_next
    surface_height = from_grid(solution, barotropic_map)
    return new_tracers, surface_height
```

```python
import functools

import jax
import jax.numpy as jnp
from jax import lax
from jax.experimental import pallas as pl
from jax.experimental.pallas import tpu as pltpu
from jax.sharding import PartitionSpec as P

ITERS = 6
RESTORE = 0.5
SURFACE = 0.1
FACE_SCALE = 2.0
SHIFTS = (0.0, 2.0, 1.0, 0.4, 1.6)
PIVOT_FLOOR = 1e-11
HALO = 8
LANES = 128
FIELDS = 4
CHUNK = 256
F32 = jnp.float32
VMEM = pl.BlockSpec(memory_space=pltpu.VMEM)
SMEM = pl.BlockSpec(memory_space=pltpu.SMEM)


def params(mebibytes):
    return pltpu.CompilerParams(vmem_limit_bytes=mebibytes * 2**20)


def columns_kernel(
    tracers, speed, mixing, wet, patch, *rest
):
    out, carry_in, carry_own, carry_up, carry_low, carry_high = rest[-6:]
    levels, blocks, count, width = tracers.shape
    wet_now = wet[...]
    shape = wet_now.shape
    zero = jnp.zeros(shape, F32)
    mix_above, up_above, down_above, inverse = zero, zero, zero, zero
    for k in range(levels):
        is_wet = (k < wet_now).astype(F32)
        is_open = (k + 1 < wet_now).astype(F32)
        flow = speed[k] * is_open
        up, down = jnp.maximum(flow, 0.0), jnp.minimum(flow, 0.0)
        mix = mixing[k] * is_open
        diagonal = 1.0 + mix + mix_above
        if k == 0:
            source = RESTORE * is_wet
            diagonal = diagonal + source
        inverse = 1.0 / (diagonal - mix_above * (mix_above * inverse))
        scaled_wet = is_wet * inverse
        carry_own[k] = scaled_wet * (1.0 + down - up_above)
        carry_up[k] = scaled_wet * up
        carry_low[k] = mix * inverse
        if k == 0:
            carry_in[k] = source * inverse
            carry_high[k] = zero
        else:
            carry_in[k] = mix_above * inverse
            carry_high[k] = scaled_wet * down_above
        mix_above, up_above, down_above = mix, up, down
    tracer_ids = lax.broadcasted_iota(jnp.int32, (count, width), 0)

    def row(ref, k, b):
        return jnp.broadcast_to(ref[k, b : b + 1, :], (count, width))

    for b in range(blocks):
        above = None
        here = tracers[0, b]
        value = None
        for k in range(levels):
            result = row(carry_own, k, b) * here
            if k + 1 < levels:
                below = tracers[k + 1, b]
                result = result + row(carry_up, k, b) * below
            if k == 0:
                target = (patch[b : b + 1, :] == tracer_ids).astype(F32)
                result = result + row(carry_in, k, b) * target
            else:
                result = result - row(carry_high, k, b) * above
                result = result + row(carry_in, k, b) * value
            value = result
            if k + 1 < levels:
                out[k, b] = value
                above, here = here, below
        out[levels - 1, b] = value
        for k in range(levels - 2, -1, -1):
            value = out[k, b] + row(carry_low, k, b) * value
            out[k, b] = value


def columns(tracers, speed, mixing, wet, patch, begin, end, previous):
    levels, blocks, count, cells = tracers.shape
    start = begin // CHUNK
    steps = (end - begin) // CHUNK
    wide = pl.BlockSpec((levels, blocks, count, CHUNK), lambda i: (0, 0, 0, i + start))
    flat = pl.BlockSpec((levels, blocks, CHUNK), lambda i: (0, 0, i + start))
    thin = pl.BlockSpec((blocks, CHUNK), lambda i: (0, i + start))
    in_specs = [wide, flat, flat, thin, thin]
    operands = [tracers, speed, mixing, wet, patch]
    aliases = {}
    if previous is not None:
        in_specs.append(pl.BlockSpec(memory_space=pl.ANY))
        operands.append(previous)
        aliases = {5: 0}
    part = steps * CHUNK * blocks * levels
    return pl.pallas_call(
        columns_kernel,
        grid=(steps,),
        in_specs=in_specs,
        out_specs=wide,
        out_shape=jax.ShapeDtypeStruct(tracers.shape, F32),
        scratch_shapes=[pltpu.VMEM((levels, blocks, CHUNK), F32)] * 5,
        input_output_aliases=aliases,
        compiler_params=params(32),
        cost_estimate=pl.CostEstimate(
            flops=part * count * 10, bytes_accessed=part * (count * 8 + 8), transcendentals=0
        ),
    )(*operands)


def payload_kernel(buoyancy, wet, prior, land, out):
    levels, blocks, cells = buoyancy.shape
    rows = cells // LANES
    wet_now = wet[...]
    total = jnp.zeros(wet_now.shape, F32)
    for k in range(levels):
        total = total + (k < wet_now).astype(F32) * buoyancy[k].astype(F32)
    depth = wet_now.astype(F32)
    first = prior[...]
    for r in range(rows):
        lanes = slice(r * LANES, (r + 1) * LANES)
        out[0, :, r, :] = total[:, lanes]
        out[1, :, r, :] = depth[:, lanes]
        out[2, :, r, :] = first[:, lanes]
    out[3] = land[...].astype(F32)


def payload_of(buoyancy, wet, prior, land):
    blocks, rows, lanes = land.shape
    return pl.pallas_call(
        payload_kernel,
        in_specs=[VMEM] * 4,
        out_specs=VMEM,
        out_shape=jax.ShapeDtypeStruct((FIELDS, blocks, rows, lanes), F32),
        compiler_params=params(16),
    )(buoyancy, wet, prior, land)


def select_kernel(spread, *refs):
    parts = refs[: len(spread)]
    clinic, tropic, place, own, to_south, to_north, band = refs[len(spread) :]
    blocks, rows = own.shape[1], own.shape[2]
    band_width = band.shape[1]
    band_row, column, band_rows = place[0], place[1], place[2]
    first_slot = band_row * band_width
    for part, (hop, ref) in enumerate(zip(spread, parts)):
        holder = (column ^ hop) * blocks
        for s in range(blocks):
            slot = first_slot + holder + s
            at = clinic[slot] - first_slot
            for f in range(FIELDS - 1):
                band[f, at] = ref[f, s]
            band[FIELDS - 1, tropic[slot] - first_slot] = ref[FIELDS - 1, s]

    lane = lax.broadcasted_iota(jnp.int32, (rows, LANES), 1)

    def sides(f, at, rows_from, rows_to):
        east = lax.rem(at + 1, band_width)
        west = lax.rem(at + band_width - 1, band_width)
        pick = lane[rows_from:rows_to]
        return jnp.where(
            pick < HALO,
            band[f, east, rows_from:rows_to],
            jnp.where(pick >= LANES - HALO, band[f, west, rows_from:rows_to], 0.0),
        )

    for i in range(blocks):
        at = tropic[first_slot + column * blocks + i] - first_slot
        for f in range(FIELDS):
            own[f, i, :, 0:LANES] = band[f, at]
            own[f, i, :, LANES : 2 * LANES] = sides(f, at, 0, rows)

    for out, move, rows_from in ((to_south, 1, rows - HALO), (to_north, -1, 0)):
        other = lax.rem(band_row + move + band_rows, band_rows) * band_width
        packed = [None] * FIELDS
        for i in range(blocks):
            at = tropic[other + column * blocks + i] - other
            for f in range(FIELDS):
                out[f, i] = band[f, at, rows_from : rows_from + HALO]
                beside = sides(f, at, rows_from, rows_from + HALO)
                if i:
                    beside = pltpu.roll(beside, 2 * HALO * i, 1)
                packed[f] = beside if i == 0 else packed[f] + beside
        for f in range(FIELDS):
            out[f, blocks] = packed[f]


def select(spread, parts, clinic, tropic, place, band_width):
    blocks, rows, lanes = parts[0].shape[1:]
    edge = jax.ShapeDtypeStruct((FIELDS, blocks + 1, HALO, lanes), F32)
    return pl.pallas_call(
        functools.partial(select_kernel, spread),
        in_specs=[VMEM] * len(parts) + [SMEM] * 3,
        out_specs=[VMEM] * 3,
        out_shape=[jax.ShapeDtypeStruct((FIELDS, blocks, rows, 2 * lanes), F32), edge, edge],
        scratch_shapes=[pltpu.VMEM((FIELDS, band_width, rows, lanes), F32)],
        compiler_params=params(16),
    )(*parts, clinic, tropic, place)


def two_sum(a, b):
    total = a + b
    part = total - a
    return total, (a - (total - part)) + (b - part)


def split(a):
    scaled = a * 4097.0
    high = scaled - (scaled - a)
    return high, a - high


def pair_add(a, b):
    high, low = two_sum(a[0], b[0])
    low = low + (a[1] + b[1])
    total = high + low
    return total, low - (total - high)


def product(a, b):
    value = a * b
    a_high, a_low = split(a)
    b_high, b_low = split(b)
    error = ((a_high * b_high - value) + a_high * b_low + a_low * b_high) + a_low * b_low
    return value, error


def pair_mul(a, b):
    value, error = product(a[0], b[0])
    error = error + (a[0] * b[1] + a[1] * b[0])
    total = value + error
    return total, error - (total - value)


def pair_inverse(a):
    guess = 1.0 / a[0]
    value, error = product(guess, a[0])
    rest = (1.0 - value) - error - guess * a[1]
    low = guess * rest
    total = guess + low
    return total, low - (total - guess)


def fold(pair, axis, steps):
    for step in steps:
        pair = pair_add(pair, tuple(pltpu.roll(part, step, axis) for part in pair))
    return pair


def basis_kernel(levels, own, north, south, vectors, guess, sums, images):
    blocks, rows = own.shape[1], own.shape[2]
    tall = rows + 2 * HALO
    inner = slice(HALO, HALO + rows)
    lane = lax.broadcasted_iota(jnp.int32, (HALO, LANES), 1)
    beside = (lane < HALO) | (lane >= LANES - HALO)

    def edge(ref, f, i):
        packed = ref[f, blocks]
        if i:
            packed = pltpu.roll(packed, LANES - 2 * HALO * i, 1)
        return jnp.concatenate([ref[f, i], jnp.where(beside, packed, 0.0)], axis=1)

    def east(v):
        return pltpu.roll(v, 2 * LANES - 1, 1)

    def west(v):
        return pltpu.roll(v, 1, 1)

    def below(v):
        return pltpu.roll(v, tall - 1, 0)

    def above(v):
        return pltpu.roll(v, 1, 0)

    for i in range(blocks):
        forcing, depth, prior, ocean = (
            jnp.concatenate([edge(north, f, i), own[f, i], edge(south, f, i)], axis=0)
            for f in range(FIELDS)
        )
        scale = FACE_SCALE / levels
        east_face = scale * jnp.minimum(depth, east(depth)) * ocean * east(ocean)
        west_face = west(east_face)
        south_face = scale * jnp.minimum(depth, below(depth)) * ocean * below(ocean)
        north_face = above(south_face)
        centre = SURFACE * ocean + (1.0 - ocean)
        diagonal = centre + east_face + west_face + south_face + north_face
        inverse = 1.0 / diagonal

        def operate(v):
            result = centre * v + east_face * (v - east(v))
            result = result + west_face * (v - west(v))
            result = result + south_face * (v - below(v))
            return result + north_face * (v - above(v))

        first = ocean * prior
        residual = ocean * forcing - operate(first)
        v = residual * inverse
        guess[i] = first[inner, 0:LANES]
        place = slice(i * rows, (i + 1) * rows)
        images[ITERS, place] = residual[inner, 0:LANES]
        for k in range(ITERS):
            image = operate(v)
            vectors[k, place] = v[inner, 0:LANES]
            images[k, place] = image[inner, 0:LANES]
            if k + 1 < ITERS:
                following = image * inverse
                v = following - SHIFTS[k] * v if SHIFTS[k] else following

    row_id = lax.broadcasted_iota(jnp.int32, (8, LANES), 0)
    lane_id = lax.broadcasted_iota(jnp.int32, (8, LANES), 1)
    entries = [(a, b) for a in range(ITERS) for b in range(a, ITERS + 1)]
    spots = [(8 * a + b, 8 * b + a if b < ITERS else -1) for a, b in entries]
    placed = None
    for begin in range(0, len(entries), 8):
        packed = (jnp.zeros((8, LANES), F32),) * 2
        spot = jnp.full((8, LANES), -1, jnp.int32)
        twin = jnp.full((8, LANES), -1, jnp.int32)
        for offset, (a, b) in enumerate(entries[begin : begin + 8]):
            total = error = None
            for r in range(0, blocks * rows, 8):
                value, rest = product(vectors[a, r : r + 8], images[b, r : r + 8])
                if total is None:
                    total, error = value, rest
                else:
                    total, extra = two_sum(total, value)
                    error = error + (rest + extra)
            pair = fold((total, error), 0, (4, 2, 1))
            mine = row_id == offset
            packed = tuple(jnp.where(mine, new, old) for new, old in zip(pair, packed))
            spot = jnp.where(mine, spots[begin + offset][0], spot)
            twin = jnp.where(mine, spots[begin + offset][1], twin)
        packed = fold(packed, 1, (64, 32, 16, 8, 4, 2, 1))
        high = jnp.where((lane_id == spot) | (lane_id == twin), packed[0], 0.0)
        low = jnp.where((lane_id == spot + 64) | ((lane_id == twin + 64) & (twin >= 0)), packed[1], 0.0)
        placed = high + low if placed is None else placed + high + low
    for step in (4, 2, 1):
        placed = placed + pltpu.roll(placed, step, 0)
    sums[...] = jnp.broadcast_to(placed[None], sums.shape)


def basis(levels, own, north, south, devices):
    fields, blocks, rows, _ = own.shape
    return pl.pallas_call(
        functools.partial(basis_kernel, levels),
        in_specs=[VMEM] * 3,
        out_specs=[VMEM] * 3,
        out_shape=[
            jax.ShapeDtypeStruct((ITERS, blocks * rows, LANES), F32),
            jax.ShapeDtypeStruct((blocks, rows, LANES), F32),
            jax.ShapeDtypeStruct((devices, 8, LANES), F32),
        ],
        scratch_shapes=[pltpu.VMEM((ITERS + 1, blocks * rows, LANES), F32)],
        compiler_params=params(16),
    )(own, north, south)


def finish_kernel(sums, vectors, guess, out):
    devices = sums.shape[0]
    blocks, rows = guess.shape[0], guess.shape[1]
    pairs = [(sums[d], jnp.zeros((8, LANES), F32)) for d in range(devices)]
    while len(pairs) > 1:
        pairs = [pair_add(pairs[j], pairs[j + 1]) for j in range(0, len(pairs), 2)]
    total, error = pairs[0]
    low = error + pltpu.roll(total, 64, 1)
    row_id = lax.broadcasted_iota(jnp.int32, (8, LANES), 0)
    lane_id = lax.broadcasted_iota(jnp.int32, (8, LANES), 1)
    keep = (row_id < ITERS) & (lane_id < ITERS + 1)

    def rows_of(vector):
        moved = vector
        for i in range(1, ITERS):
            moved = jnp.where(row_id == i, pltpu.roll(vector, LANES - 8 * i, 1), moved)
        return jnp.where(keep, moved, 0.0)

    matrix = (rows_of(total), rows_of(low))
    energy = matrix[0]
    for k in range(ITERS):
        column = tuple(jnp.broadcast_to(part[:, k : k + 1], (8, LANES)) for part in matrix)
        pivot_row = tuple(jnp.broadcast_to(part[k : k + 1, :], (8, LANES)) for part in matrix)
        pivot = tuple(jnp.broadcast_to(part[k : k + 1, :], (8, LANES)) for part in column)
        full = jnp.broadcast_to(energy[k : k + 1, k : k + 1], (8, LANES))
        good = pivot[0] > PIVOT_FLOOR * full
        safe = (jnp.where(good, pivot[0], 1.0), jnp.where(good, pivot[1], 0.0))
        inverse = tuple(jnp.where(good, part, 0.0) for part in pair_inverse(safe))
        scaled = pair_mul(pivot_row, inverse)
        change = pair_mul(column, scaled)
        moved = pair_add(matrix, (-change[0], -change[1]))
        matrix = tuple(
            jnp.where(row_id == k, new, jnp.where(keep, old, 0.0)) for new, old in zip(scaled, moved)
        )
    weights = matrix[0]
    result = guess[...]
    for k in range(ITERS):
        weight = jnp.broadcast_to(weights[k : k + 1, ITERS : ITERS + 1], (rows, LANES))
        result = result + weight[None] * vectors[k].reshape(blocks, rows, LANES)
    out[...] = result


def finish(sums, vectors, guess):
    return pl.pallas_call(
        finish_kernel,
        in_specs=[VMEM] * 3,
        out_specs=VMEM,
        out_shape=jax.ShapeDtypeStruct(guess.shape, F32),
        compiler_params=params(16),
    )(sums, vectors, guess)


def swap(array, axis, hop):
    count = lax.axis_size(axis)
    return lax.ppermute(array, axis, [(i, i ^ hop) for i in range(count)])


def local(
    tracers,
    vertical_speed,
    diffusivity,
    buoyancy_force,
    wet_levels,
    surface_patch,
    prior_height,
    land_mask,
    baroclinic_map,
    barotropic_map,
):
    levels, blocks, _, cells = tracers.shape
    band_rows, holders = lax.axis_size("by"), lax.axis_size("bx")
    place = jnp.stack(
        [lax.axis_index("by"), lax.axis_index("bx"), jnp.int32(band_rows)]
    ).astype(jnp.int32)

    payload = payload_of(buoyancy_force, wet_levels, prior_height, land_mask)
    spread = list(range(0, holders, 2))
    parts = [payload] + [swap(payload, "bx", hop) for hop in spread[1:]]
    parts = parts + [swap(part, "bx", 1) for part in parts]
    spread = spread + [hop + 1 for hop in spread]

    own, to_south, to_north = select(
        tuple(spread), parts, baroclinic_map, barotropic_map, place, holders * blocks
    )
    north = lax.ppermute(to_south, "by", [(i, i + 1) for i in range(band_rows - 1)])
    south = lax.ppermute(to_north, "by", [(i + 1, i) for i in range(band_rows - 1)])

    half = cells // 2
    stepped = columns(
        tracers, vertical_speed, diffusivity, wet_levels, surface_patch, 0, half, None
    )
    stepped = columns(
        tracers, vertical_speed, diffusivity, wet_levels, surface_patch, half, cells, stepped
    )

    vectors, guess, sums = basis(levels, own, north, south, band_rows * holders)
    gathered = lax.all_to_all(sums, ("by", "bx"), 0, 0, tiled=True)
    return stepped, finish(gathered, vectors, guess)


def solution(mesh):
    slots = ("by", "bx")
    return jax.shard_map(
        local,
        mesh=mesh,
        in_specs=(
            P(None, slots, None, None),
            P(None, slots, None),
            P(None, slots, None),
            P(None, slots, None),
            P(slots, None),
            P(slots, None),
            P(slots, None),
            P(slots, None, None),
            P(),
            P(),
        ),
        out_specs=(P(None, slots, None, None), P(slots, None, None)),
        check_vma=False,
    )
```

```python
import functools

import jax
import jax.numpy as jnp
from jax import lax
from jax.experimental import pallas as pl
from jax.experimental.pallas import tpu as pltpu
from jax.sharding import PartitionSpec as P

ITERS = 6
RESTORE = 0.5
SURFACE = 0.1
FACE_SCALE = 2.0
SHIFTS = (0.0, 2.0, 1.0, 0.4, 1.6)
PIVOT_FLOOR = 1e-11
HALO = 8
LANES = 128
FIELDS = 4
CHUNK = 512
EARLY = 4
F32 = jnp.float32
VMEM = pl.BlockSpec(memory_space=pltpu.VMEM)
SMEM = pl.BlockSpec(memory_space=pltpu.SMEM)
HBM = pl.BlockSpec(memory_space=pltpu.HBM)


def in_hbm(*arrays):
    return [pltpu.with_memory_space_constraint(array, pltpu.HBM) for array in arrays]


def params(mebibytes):
    return pltpu.CompilerParams(vmem_limit_bytes=mebibytes * 2**20)


def columns_step(tracers, speed, mixing, wet, patch, out, carry_in, carry_own, carry_up, carry_low, carry_high):
    levels, blocks, count, width = tracers.shape
    tiles = width // LANES

    def stacked(block):
        return jnp.concatenate([block[:, t * LANES : (t + 1) * LANES] for t in range(tiles)], axis=0)

    wet_now = stacked(wet[...])
    zero = jnp.zeros(wet_now.shape, F32)
    mix_above, up_above, down_above, inverse = zero, zero, zero, zero
    for k in range(levels):
        is_wet = (k < wet_now).astype(F32)
        is_open = (k + 1 < wet_now).astype(F32)
        flow = stacked(speed[k]) * is_open
        up, down = jnp.maximum(flow, 0.0), jnp.minimum(flow, 0.0)
        mix = stacked(mixing[k]) * is_open
        diagonal = 1.0 + mix + mix_above
        if k == 0:
            source = RESTORE * is_wet
            diagonal = diagonal + source
        inverse = 1.0 / (diagonal - mix_above * (mix_above * inverse))
        scaled_wet = is_wet * inverse
        carry_own[k] = scaled_wet * (1.0 + down - up_above)
        carry_up[k] = scaled_wet * up
        carry_low[k] = mix * inverse
        if k == 0:
            carry_in[k] = source * inverse
            carry_high[k] = zero
        else:
            carry_in[k] = mix_above * inverse
            carry_high[k] = scaled_wet * down_above
        mix_above, up_above, down_above = mix, up, down
    tracer_ids = lax.broadcasted_iota(jnp.int32, (count, LANES), 0)

    for b in range(blocks):
        for t in range(tiles):
            lanes = slice(t * LANES, (t + 1) * LANES)
            at = t * blocks + b

            def row(ref, k):
                return jnp.broadcast_to(ref[k, at : at + 1, :], (count, LANES))

            above = value = None
            here = tracers[0, b, :, lanes]
            for k in range(levels):
                result = row(carry_own, k) * here
                if k + 1 < levels:
                    below = tracers[k + 1, b, :, lanes]
                    result = result + row(carry_up, k) * below
                if k == 0:
                    target = (patch[b : b + 1, lanes] == tracer_ids).astype(F32)
                    result = result + row(carry_in, k) * target
                else:
                    result = result - row(carry_high, k) * above
                    result = result + row(carry_in, k) * value
                value = result
                if k + 1 < levels:
                    out[k, b, :, lanes] = value
                    above, here = here, below
            out[levels - 1, b, :, lanes] = value
            for k in range(levels - 2, -1, -1):
                value = out[k, b, :, lanes] + row(carry_low, k) * value
                out[k, b, :, lanes] = value


def columns_kernel(start, steps, operands, *refs):
    inputs = refs[:5]
    out, mark = refs[operands], refs[operands + 1]
    scratch = refs[operands + 2 :]
    levels, blocks, count, _ = out.shape
    wide = pl.BlockSpec((levels, blocks, count, CHUNK), lambda i: (0, 0, 0, i + start))
    flat = pl.BlockSpec((levels, blocks, CHUNK), lambda i: (0, 0, i + start))
    thin = pl.BlockSpec((blocks, CHUNK), lambda i: (0, i + start))

    def body(*blocks_now):
        columns_step(*blocks_now, *scratch)

    pltpu.emit_pipeline(
        body, grid=(steps,), in_specs=[wide, flat, flat, thin, thin], out_specs=[wide]
    )(*inputs, out)
    mark[...] = jnp.zeros(mark.shape, F32)


def columns(tracers, speed, mixing, wet, patch, begin, end, previous, after):
    levels, blocks, count, cells = tracers.shape
    operands = in_hbm(tracers, speed, mixing, wet, patch) + [after]
    aliases = {}
    if previous is not None:
        aliases = {len(operands): 0}
        operands += in_hbm(previous)
    part = (end - begin) * CHUNK * blocks * levels
    tall = CHUNK // LANES * blocks
    return pl.pallas_call(
        functools.partial(columns_kernel, begin, end - begin, len(operands)),
        in_specs=[HBM] * 5 + [pl.BlockSpec(memory_space=pl.ANY)] + [HBM] * len(aliases),
        out_specs=[HBM, VMEM],
        out_shape=[
            jax.ShapeDtypeStruct(tracers.shape, F32),
            jax.ShapeDtypeStruct((8, LANES), F32),
        ],
        scratch_shapes=[pltpu.VMEM((levels, tall, LANES), F32)] * 5,
        input_output_aliases=aliases,
        compiler_params=params(32),
        cost_estimate=pl.CostEstimate(
            flops=part * count * 10, bytes_accessed=part * (count * 8 + 8), transcendentals=0
        ),
    )(*operands)


def payload_kernel(buoyancy, wet, prior, land, clinic, tropic, out, clinic_out, tropic_out, force, wet_in, prior_in, land_in, sems):
    copies = [
        pltpu.make_async_copy(source, target, sems.at[j])
        for j, (source, target) in enumerate(
            (
                (buoyancy, force),
                (wet, wet_in),
                (prior, prior_in),
                (land, land_in),
                (clinic, clinic_out),
                (tropic, tropic_out),
            )
        )
    ]
    for copy in copies:
        copy.start()
    for copy in copies:
        copy.wait()
    levels, blocks, cells = force.shape
    rows = cells // LANES
    wet_now = wet_in[...]
    total = jnp.zeros(wet_now.shape, F32)
    for k in range(levels):
        total = total + (k < wet_now).astype(F32) * force[k].astype(F32)
    depth = wet_now.astype(F32)
    first = prior_in[...]
    for r in range(rows):
        lanes = slice(r * LANES, (r + 1) * LANES)
        out[0, :, r, :] = total[:, lanes]
        out[1, :, r, :] = depth[:, lanes]
        out[2, :, r, :] = first[:, lanes]
    out[3] = land_in[...].astype(F32)


def payload_of(buoyancy, wet, prior, land, clinic, tropic):
    blocks, rows, lanes = land.shape
    return pl.pallas_call(
        payload_kernel,
        in_specs=[HBM] * 6,
        out_specs=[VMEM] * 3,
        out_shape=[
            jax.ShapeDtypeStruct((FIELDS, blocks, rows, lanes), F32),
            jax.ShapeDtypeStruct(clinic.shape, clinic.dtype),
            jax.ShapeDtypeStruct(tropic.shape, tropic.dtype),
        ],
        scratch_shapes=[
            pltpu.VMEM(each.shape, each.dtype) for each in (buoyancy, wet, prior, land)
        ]
        + [pltpu.SemaphoreType.DMA((6,))],
        compiler_params=params(16),
    )(*in_hbm(buoyancy, wet, prior, land, clinic, tropic))


def select_kernel(spread, band_rows, *refs):
    parts = refs[: len(spread)]
    clinic, tropic, _, own, to_pair, to_other, band = refs[len(spread) :]
    blocks = own.shape[1]
    band_width = band.shape[1]
    band_row, column = lax.axis_index("by"), lax.axis_index("bx")
    first_slot = band_row * band_width
    for hop, ref in zip(spread, parts):
        holder = (column ^ hop) * blocks
        for s in range(blocks):
            slot = first_slot + holder + s
            at = clinic[slot] - first_slot
            for f in range(FIELDS - 1):
                for h in range(2):
                    band[f, at, h] = ref[f, s, h * HALO : (h + 1) * HALO]
            at = tropic[slot] - first_slot
            for h in range(2):
                band[FIELDS - 1, at, h] = ref[FIELDS - 1, s, h * HALO : (h + 1) * HALO]

    lane = lax.broadcasted_iota(jnp.int32, (HALO, LANES), 1)

    def sides(f, at, half):
        east = lax.rem(at + 1, band_width)
        west = lax.rem(at + band_width - 1, band_width)
        return jnp.where(
            lane < HALO,
            band[f, east, half],
            jnp.where(lane >= LANES - HALO, band[f, west, half], 0.0),
        )

    for i in range(blocks):
        at = tropic[first_slot + column * blocks + i] - first_slot
        for f in range(FIELDS):
            for h in range(2):
                rows = slice(h * HALO, (h + 1) * HALO)
                own[f, i, rows, 0:LANES] = band[f, at, h]
                own[f, i, rows, LANES : 2 * LANES] = sides(f, at, h)

    odd = lax.rem(band_row, 2)
    for out, move in ((to_pair, 1 - 2 * odd), (to_other, 2 * odd - 1)):
        half = (move + 1) // 2
        other = lax.rem(band_row + move + band_rows, band_rows) * band_width
        packed = [None] * FIELDS
        for i in range(blocks):
            at = tropic[other + column * blocks + i] - other
            for f in range(FIELDS):
                out[f, i] = band[f, at, half]
                beside = sides(f, at, half)
                if i:
                    beside = pltpu.roll(beside, 2 * HALO * i, 1)
                packed[f] = beside if i == 0 else packed[f] + beside
        for f in range(FIELDS):
            out[f, blocks] = packed[f]


def select(spread, band_rows, parts, clinic, tropic, band_width, after):
    blocks, rows, lanes = parts[0].shape[1:]
    assert 2 * HALO * blocks <= LANES
    edge = jax.ShapeDtypeStruct((FIELDS, blocks + 1, HALO, lanes), F32)
    return pl.pallas_call(
        functools.partial(select_kernel, spread, band_rows),
        in_specs=[VMEM] * len(parts) + [SMEM] * 2 + [pl.BlockSpec(memory_space=pl.ANY)],
        out_specs=[VMEM] * 3,
        out_shape=[jax.ShapeDtypeStruct((FIELDS, blocks, rows, 2 * lanes), F32), edge, edge],
        scratch_shapes=[pltpu.VMEM((FIELDS, band_width, rows // HALO, HALO, lanes), F32)],
        compiler_params=params(16),
    )(*parts, clinic, tropic, after)


def two_sum(a, b):
    total = a + b
    part = total - a
    return total, (a - (total - part)) + (b - part)


def split(a):
    scaled = a * 4097.0
    high = scaled - (scaled - a)
    return high, a - high


def pair_add(a, b):
    high, low = two_sum(a[0], b[0])
    low = low + (a[1] + b[1])
    total = high + low
    return total, low - (total - high)


def product(a, b):
    value = a * b
    a_high, a_low = split(a)
    b_high, b_low = split(b)
    error = ((a_high * b_high - value) + a_high * b_low + a_low * b_high) + a_low * b_low
    return value, error


def pair_mul(a, b):
    value, error = product(a[0], b[0])
    error = error + (a[0] * b[1] + a[1] * b[0])
    total = value + error
    return total, error - (total - value)


def pair_inverse(a):
    guess = 1.0 / a[0]
    value, error = product(guess, a[0])
    rest = (1.0 - value) - error - guess * a[1]
    low = guess * rest
    total = guess + low
    return total, low - (total - guess)


def fold(pair, axis, steps):
    for step in steps:
        pair = pair_add(pair, tuple(pltpu.roll(part, step, axis) for part in pair))
    return pair


def basis_kernel(levels, band_rows, own, from_pair, from_other, vectors, guess, sums, images):
    blocks, rows = own.shape[1], own.shape[2]
    tall = rows + 2 * HALO
    inner = slice(HALO, HALO + rows)
    lane = lax.broadcasted_iota(jnp.int32, (HALO, LANES), 1)
    beside = (lane < HALO) | (lane >= LANES - HALO)

    band_row = lax.axis_index("by")
    odd = lax.rem(band_row, 2) == 1

    def edge(from_odd, from_even, present, f, i):
        packed = jnp.where(odd, from_odd[f, blocks], from_even[f, blocks])
        if i:
            packed = pltpu.roll(packed, LANES - 2 * HALO * i, 1)
        middle = jnp.where(odd, from_odd[f, i], from_even[f, i])
        both = jnp.concatenate([middle, jnp.where(beside, packed, 0.0)], axis=1)
        return jnp.where(present, both, 0.0)

    def east(v):
        return pltpu.roll(v, 2 * LANES - 1, 1)

    def west(v):
        return pltpu.roll(v, 1, 1)

    def below(v):
        return pltpu.roll(v, tall - 1, 0)

    def above(v):
        return pltpu.roll(v, 1, 0)

    for i in range(blocks):
        forcing, depth, prior, ocean = (
            jnp.concatenate(
                [
                    edge(from_pair, from_other, band_row > 0, f, i),
                    own[f, i],
                    edge(from_other, from_pair, band_row < band_rows - 1, f, i),
                ],
                axis=0,
            )
            for f in range(FIELDS)
        )
        scale = FACE_SCALE / levels
        east_face = scale * jnp.minimum(depth, east(depth)) * ocean * east(ocean)
        west_face = west(east_face)
        south_face = scale * jnp.minimum(depth, below(depth)) * ocean * below(ocean)
        north_face = above(south_face)
        centre = SURFACE * ocean + (1.0 - ocean)
        diagonal = centre + east_face + west_face + south_face + north_face
        inverse = 1.0 / diagonal

        def operate(v):
            result = centre * v + east_face * (v - east(v))
            result = result + west_face * (v - west(v))
            result = result + south_face * (v - below(v))
            return result + north_face * (v - above(v))

        first = ocean * prior
        residual = ocean * forcing - operate(first)
        v = residual * inverse
        guess[i] = first[inner, 0:LANES]
        place = slice(i * rows, (i + 1) * rows)
        images[ITERS, place] = residual[inner, 0:LANES]
        for k in range(ITERS):
            image = operate(v)
            vectors[k, place] = v[inner, 0:LANES]
            images[k, place] = image[inner, 0:LANES]
            if k + 1 < ITERS:
                following = image * inverse
                v = following - SHIFTS[k] * v if SHIFTS[k] else following

    row_id = lax.broadcasted_iota(jnp.int32, (8, LANES), 0)
    lane_id = lax.broadcasted_iota(jnp.int32, (8, LANES), 1)
    entries = [(a, b) for a in range(ITERS) for b in range(a, ITERS + 1)]
    spots = [(8 * a + b, 8 * b + a if b < ITERS else -1) for a, b in entries]
    placed = None
    for begin in range(0, len(entries), 8):
        packed = (jnp.zeros((8, LANES), F32),) * 2
        spot = jnp.full((8, LANES), -1, jnp.int32)
        twin = jnp.full((8, LANES), -1, jnp.int32)
        for offset, (a, b) in enumerate(entries[begin : begin + 8]):
            total = error = None
            for r in range(0, blocks * rows, 8):
                value, rest = product(vectors[a, r : r + 8], images[b, r : r + 8])
                if total is None:
                    total, error = value, rest
                else:
                    total, extra = two_sum(total, value)
                    error = error + (rest + extra)
            pair = fold((total, error), 0, (4, 2, 1))
            mine = row_id == offset
            packed = tuple(jnp.where(mine, new, old) for new, old in zip(pair, packed))
            spot = jnp.where(mine, spots[begin + offset][0], spot)
            twin = jnp.where(mine, spots[begin + offset][1], twin)
        packed = fold(packed, 1, (64, 32, 16, 8, 4, 2, 1))
        high = jnp.where((lane_id == spot) | (lane_id == twin), packed[0], 0.0)
        low = jnp.where((lane_id == spot + 64) | ((lane_id == twin + 64) & (twin >= 0)), packed[1], 0.0)
        placed = high + low if placed is None else placed + high + low
    for step in (4, 2, 1):
        placed = placed + pltpu.roll(placed, step, 0)
    sums[...] = jnp.broadcast_to(placed[0:1][None], sums.shape)


def basis(levels, own, from_pair, from_other, band_rows, devices):
    fields, blocks, rows, _ = own.shape
    return pl.pallas_call(
        functools.partial(basis_kernel, levels, band_rows),
        in_specs=[VMEM] * 3,
        out_specs=[VMEM] * 3,
        out_shape=[
            jax.ShapeDtypeStruct((ITERS, blocks * rows, LANES), F32),
            jax.ShapeDtypeStruct((blocks, rows, LANES), F32),
            jax.ShapeDtypeStruct((devices, 1, LANES), F32),
        ],
        scratch_shapes=[pltpu.VMEM((ITERS + 1, blocks * rows, LANES), F32)],
        compiler_params=params(16),
    )(own, from_pair, from_other)


def finish_kernel(sums, vectors, guess, out):
    devices = sums.shape[0]
    blocks, rows = guess.shape[0], guess.shape[1]
    pairs = [(sums[d : d + 8], jnp.zeros((8, LANES), F32)) for d in range(0, devices, 8)]
    while len(pairs) > 1:
        pairs = [pair_add(pairs[j], pairs[j + 1]) for j in range(0, len(pairs), 2)]
    total, error = fold(pairs[0], 0, (4, 2, 1))
    low = error + pltpu.roll(total, 64, 1)
    row_id = lax.broadcasted_iota(jnp.int32, (8, LANES), 0)
    lane_id = lax.broadcasted_iota(jnp.int32, (8, LANES), 1)
    keep = (row_id < ITERS) & (lane_id < ITERS + 1)

    def rows_of(vector):
        moved = vector
        for i in range(1, ITERS):
            moved = jnp.where(row_id == i, pltpu.roll(vector, LANES - 8 * i, 1), moved)
        return jnp.where(keep, moved, 0.0)

    matrix = (rows_of(total), rows_of(low))
    energy = matrix[0]
    for k in range(ITERS):
        column = tuple(jnp.broadcast_to(part[:, k : k + 1], (8, LANES)) for part in matrix)
        pivot_row = tuple(jnp.broadcast_to(part[k : k + 1, :], (8, LANES)) for part in matrix)
        pivot = tuple(jnp.broadcast_to(part[k : k + 1, :], (8, LANES)) for part in column)
        full = jnp.broadcast_to(energy[k : k + 1, k : k + 1], (8, LANES))
        good = pivot[0] > PIVOT_FLOOR * full
        safe = (jnp.where(good, pivot[0], 1.0), jnp.where(good, pivot[1], 0.0))
        inverse = tuple(jnp.where(good, part, 0.0) for part in pair_inverse(safe))
        scaled = pair_mul(pivot_row, inverse)
        change = pair_mul(column, scaled)
        moved = pair_add(matrix, (-change[0], -change[1]))
        matrix = tuple(
            jnp.where(row_id == k, new, jnp.where(keep, old, 0.0)) for new, old in zip(scaled, moved)
        )
    weights = matrix[0]
    result = guess[...]
    for k in range(ITERS):
        weight = jnp.broadcast_to(weights[k : k + 1, ITERS : ITERS + 1], (rows, LANES))
        result = result + weight[None] * vectors[k].reshape(blocks, rows, LANES)
    out[...] = result


def finish(sums, vectors, guess):
    return pl.pallas_call(
        finish_kernel,
        in_specs=[VMEM] * 3,
        out_specs=VMEM,
        out_shape=jax.ShapeDtypeStruct(guess.shape, F32),
        compiler_params=params(16),
    )(sums, vectors, guess)


def swap(array, axis, hop):
    count = lax.axis_size(axis)
    return lax.ppermute(array, axis, [(i, i ^ hop) for i in range(count)])


def other_partners(band_rows, holders):
    pairs = []
    for row in range(band_rows):
        other = ((row + 1) ^ 1) - 1
        for column in range(holders):
            inside = 0 <= other < band_rows
            target = (other, column) if inside else (row, column ^ 1)
            pairs.append((row * holders + column, target[0] * holders + target[1]))
    return pairs


def local(
    tracers,
    vertical_speed,
    diffusivity,
    buoyancy_force,
    wet_levels,
    surface_patch,
    prior_height,
    land_mask,
    baroclinic_map,
    barotropic_map,
):
    levels, blocks, _, cells = tracers.shape
    band_rows, holders = lax.axis_size("by"), lax.axis_size("bx")
    chunks = cells // CHUNK
    early = chunks * EARLY // 8
    column_inputs = (tracers, vertical_speed, diffusivity, wet_levels, surface_patch)

    payload, clinic, tropic = payload_of(
        buoyancy_force, wet_levels, prior_height, land_mask, baroclinic_map, barotropic_map
    )
    spread = list(range(0, holders, 2))
    parts = [payload] + [swap(payload, "bx", hop) for hop in spread[1:]]
    stepped, mark = columns(*column_inputs, 0, early, None, payload)
    *parts, mark = lax.optimization_barrier((*parts, mark))
    parts = parts + [swap(part, "bx", 1) for part in parts]
    spread = spread + [hop + 1 for hop in spread]

    own, to_pair, to_other = select(
        tuple(spread), band_rows, parts, clinic, tropic, holders * blocks, mark
    )
    from_pair = swap(to_pair, "by", 1)
    from_other = lax.ppermute(to_other, ("by", "bx"), other_partners(band_rows, holders))
    vectors, guess, sums = basis(
        levels, own, from_pair, from_other, band_rows, band_rows * holders
    )
    gathered = lax.all_to_all(sums, ("by", "bx"), 0, 0, tiled=True)
    stepped, _ = columns(*column_inputs, early, chunks, stepped, sums)
    gathered = gathered.reshape(band_rows * holders, LANES)
    return stepped, finish(gathered, vectors, guess)


def solution(mesh):
    slots = ("by", "bx")
    return jax.shard_map(
        local,
        mesh=mesh,
        in_specs=(
            P(None, slots, None, None),
            P(None, slots, None),
            P(None, slots, None),
            P(None, slots, None),
            P(slots, None),
            P(slots, None),
            P(slots, None),
            P(slots, None, None),
            P(),
            P(),
        ),
        out_specs=(P(None, slots, None, None), P(slots, None, None)),
        check_vma=False,
    )
```

```python
import functools

import jax
import jax.numpy as jnp
from jax import lax
from jax.experimental import pallas as pl
from jax.experimental.pallas import tpu as pltpu
from jax.sharding import PartitionSpec as P

ITERS = 6
RESTORE = 0.5
SURFACE = 0.1
FACE_SCALE = 2.0
SHIFTS = (0.0, 2.0, 1.0, 0.4, 1.6)
PIVOT_FLOOR = 1e-11
HALO = 8
LANES = 128
FIELDS = 4
ENTRIES = [(a, b) for a in range(ITERS) for b in range(a, ITERS + 1)]
CHUNK = 512
EARLY = 9
F32 = jnp.float32
VMEM = pl.BlockSpec(memory_space=pltpu.VMEM)
SMEM = pl.BlockSpec(memory_space=pltpu.SMEM)
HBM = pl.BlockSpec(memory_space=pltpu.HBM)


def in_hbm(*arrays):
    return [pltpu.with_memory_space_constraint(array, pltpu.HBM) for array in arrays]


def params(mebibytes):
    return pltpu.CompilerParams(vmem_limit_bytes=mebibytes * 2**20)


def fold_columns(speed, mixing, wet, patch, regions, factors):
    enter, keep, raise_, lower, sink = factors
    levels = speed.shape[0]
    tiles = speed.shape[2] // LANES

    def stacked(block):
        return jnp.concatenate([block[:, t * LANES : (t + 1) * LANES] for t in range(tiles)], axis=0)

    regions[...] = stacked(patch[...])
    wet_now = stacked(wet[...])
    zero = jnp.zeros(wet_now.shape, F32)
    mix_above, up_above, down_above, inverse = zero, zero, zero, zero
    for k in range(levels):
        is_wet = (k < wet_now).astype(F32)
        is_open = (k + 1 < wet_now).astype(F32)
        flow = stacked(speed[k]) * is_open
        up, down = jnp.maximum(flow, 0.0), jnp.minimum(flow, 0.0)
        mix = stacked(mixing[k]) * is_open
        diagonal = 1.0 + mix + mix_above
        if k == 0:
            source = RESTORE * is_wet
            diagonal = diagonal + source
        inverse = 1.0 / (diagonal - mix_above * (mix_above * inverse))
        scaled_wet = is_wet * inverse
        keep[k] = scaled_wet * (1.0 + down - up_above)
        raise_[k] = scaled_wet * up
        lower[k] = mix * inverse
        enter[k] = (source if k == 0 else mix_above) * inverse
        sink[k] = scaled_wet * down_above
        mix_above, up_above, down_above = mix, up, down


def sweep(begin, tracers, out, regions, factors, held, in_sems, out_sems):
    enter, keep, raise_, lower, sink = factors
    steps, levels, count, width = held.shape
    blocks = tracers.shape[1]
    tiles = width // LANES

    def place(ref, j):
        slot = lax.rem(j + begin, blocks)
        at = pl.multiple_of((j + begin) // blocks * width, width)
        return ref.at[:, slot, :, pl.ds(at, width)]

    def load(j):
        return pltpu.make_async_copy(place(tracers, j), held.at[j], in_sems.at[j])

    def store(j):
        return pltpu.make_async_copy(held.at[j], place(out, j), out_sems.at[j])

    tracer_ids = lax.broadcasted_iota(jnp.int32, (count, width), 0)

    def solve(j, carry):
        load(j).wait()
        slot = lax.rem(j + begin, blocks)
        first = (j + begin) // blocks * tiles

        def rows(take):
            return jnp.concatenate(
                [
                    jnp.broadcast_to(take(pl.ds((first + t) * blocks + slot, 1)), (count, LANES))
                    for t in range(tiles)
                ],
                axis=1,
            )

        def row(ref, k):
            return rows(lambda at: ref[k, at, :])

        above = value = None
        here = held[j, 0]
        for k in range(levels):
            result = row(keep, k) * here
            if k + 1 < levels:
                below = held[j, k + 1]
                result = result + row(raise_, k) * below
            if k == 0:
                target = (rows(lambda at: regions[at, :]) == tracer_ids).astype(F32)
                result = result + row(enter, k) * target
            else:
                result = result - row(sink, k) * above
                result = result + row(enter, k) * value
            value = result
            held[j, k] = value
            if k + 1 < levels:
                above, here = here, below
        for k in range(levels - 2, -1, -1):
            value = held[j, k] + row(lower, k) * value
            held[j, k] = value
        store(j).start()
        return carry

    def run(prepare):
        for j in range(steps):
            load(j).start()
        prepare()
        lax.fori_loop(0, steps, solve, 0)
        for j in range(steps):
            store(j).wait()

    return run


def first_columns_kernel(tracers, speed, mixing, wet, patch, after, out, mark, regions, *rest):
    factors, (held, speed_in, mixing_in, wet_in, patch_in, sems, in_sems, out_sems) = rest[:5], rest[5:]
    copies = [
        pltpu.make_async_copy(source, target, sems.at[j])
        for j, (source, target) in enumerate(
            ((speed, speed_in), (mixing, mixing_in), (wet, wet_in), (patch, patch_in))
        )
    ]
    for copy in copies:
        copy.start()

    def prepare():
        for copy in copies:
            copy.wait()
        fold_columns(speed_in, mixing_in, wet_in, patch_in, regions, factors)

    mark[...] = jnp.zeros(mark.shape, F32)
    sweep(0, tracers, out, regions, factors, held, in_sems, out_sems)(prepare)


def first_columns(tracers, speed, mixing, wet, patch, steps, after):
    levels, blocks, count, cells = tracers.shape
    rows = cells // LANES * blocks
    factor = jax.ShapeDtypeStruct((levels, rows, LANES), F32)
    return pl.pallas_call(
        first_columns_kernel,
        in_specs=[HBM] * 5 + [pl.BlockSpec(memory_space=pl.ANY)],
        out_specs=[HBM] + [VMEM] * 7,
        out_shape=[
            jax.ShapeDtypeStruct(tracers.shape, F32),
            jax.ShapeDtypeStruct((8, LANES), F32),
            jax.ShapeDtypeStruct((rows, LANES), jnp.int32),
        ]
        + [factor] * 5,
        scratch_shapes=[pltpu.VMEM((steps, levels, count, CHUNK), F32)]
        + [pltpu.VMEM(each.shape, each.dtype) for each in (speed, mixing, wet, patch)]
        + [pltpu.SemaphoreType.DMA((n,)) for n in (4, steps, steps)],
        compiler_params=params(40),
        cost_estimate=column_cost(tracers, steps),
    )(*in_hbm(tracers, speed, mixing, wet, patch), after)


def rest_columns_kernel(begin, tracers, regions, *rest):
    factors, (_, _, out, mark, held, in_sems, out_sems) = rest[:5], rest[5:]
    mark[...] = jnp.zeros(mark.shape, F32)
    sweep(begin, tracers, out, regions, factors, held, in_sems, out_sems)(lambda: None)


def rest_columns(tracers, begin, previous, regions, factors, after):
    levels, blocks, count, cells = tracers.shape
    steps = cells // CHUNK * blocks - begin
    return pl.pallas_call(
        functools.partial(rest_columns_kernel, begin),
        in_specs=[HBM] + [VMEM] * 6 + [HBM, pl.BlockSpec(memory_space=pl.ANY)],
        out_specs=[HBM, VMEM],
        out_shape=[
            jax.ShapeDtypeStruct(tracers.shape, F32),
            jax.ShapeDtypeStruct((8, LANES), F32),
        ],
        scratch_shapes=[pltpu.VMEM((steps, levels, count, CHUNK), F32)]
        + [pltpu.SemaphoreType.DMA((steps,))] * 2,
        input_output_aliases={7: 0},
        compiler_params=params(24),
        cost_estimate=column_cost(tracers, steps),
    )(*in_hbm(tracers), regions, *factors, *in_hbm(previous), after)


def column_cost(tracers, steps):
    levels, _, count, _ = tracers.shape
    part = steps * CHUNK * levels
    return pl.CostEstimate(
        flops=part * count * 10, bytes_accessed=part * (count * 8 + 8), transcendentals=0
    )


def payload_kernel(buoyancy, wet, prior, land, clinic, tropic, out, clinic_out, tropic_out, force, wet_in, prior_in, land_in, sems):
    copies = [
        pltpu.make_async_copy(source, target, sems.at[j])
        for j, (source, target) in enumerate(
            (
                (buoyancy, force),
                (wet, wet_in),
                (prior, prior_in),
                (land, land_in),
                (clinic, clinic_out),
                (tropic, tropic_out),
            )
        )
    ]
    for copy in copies:
        copy.start()
    for copy in copies:
        copy.wait()
    levels, blocks, cells = force.shape
    rows = cells // LANES
    wet_now = wet_in[...]
    total = jnp.zeros(wet_now.shape, F32)
    for k in range(levels):
        total = total + (k < wet_now).astype(F32) * force[k].astype(F32)
    depth = wet_now.astype(F32)
    first = prior_in[...]
    for r in range(rows):
        lanes = slice(r * LANES, (r + 1) * LANES)
        out[0, :, r, :] = total[:, lanes]
        out[1, :, r, :] = depth[:, lanes]
        out[2, :, r, :] = first[:, lanes]
    out[3] = land_in[...].astype(F32)


def payload_of(buoyancy, wet, prior, land, clinic, tropic):
    blocks, rows, lanes = land.shape
    return pl.pallas_call(
        payload_kernel,
        in_specs=[HBM] * 6,
        out_specs=[VMEM] * 3,
        out_shape=[
            jax.ShapeDtypeStruct((FIELDS, blocks, rows, lanes), F32),
            jax.ShapeDtypeStruct(clinic.shape, clinic.dtype),
            jax.ShapeDtypeStruct(tropic.shape, tropic.dtype),
        ],
        scratch_shapes=[
            pltpu.VMEM(each.shape, each.dtype) for each in (buoyancy, wet, prior, land)
        ]
        + [pltpu.SemaphoreType.DMA((6,))],
        compiler_params=params(16),
    )(*in_hbm(buoyancy, wet, prior, land, clinic, tropic))


def select_kernel(spread, band_rows, *refs):
    parts = refs[: len(spread)]
    clinic, tropic, _, own, to_pair, to_other, band = refs[len(spread) :]
    blocks = own.shape[1]
    band_width = band.shape[1]
    band_row, column = lax.axis_index("by"), lax.axis_index("bx")
    first_slot = band_row * band_width
    for hop, ref in zip(spread, parts):
        holder = (column ^ hop) * blocks
        for s in range(blocks):
            slot = first_slot + holder + s
            at = clinic[slot] - first_slot
            for f in range(FIELDS - 1):
                for h in range(2):
                    band[f, at, h] = ref[f, s, h * HALO : (h + 1) * HALO]
            at = tropic[slot] - first_slot
            for h in range(2):
                band[FIELDS - 1, at, h] = ref[FIELDS - 1, s, h * HALO : (h + 1) * HALO]

    lane = lax.broadcasted_iota(jnp.int32, (HALO, LANES), 1)

    def sides(f, at, half):
        east = lax.rem(at + 1, band_width)
        west = lax.rem(at + band_width - 1, band_width)
        return jnp.where(
            lane < HALO,
            band[f, east, half],
            jnp.where(lane >= LANES - HALO, band[f, west, half], 0.0),
        )

    for i in range(blocks):
        at = tropic[first_slot + column * blocks + i] - first_slot
        for f in range(FIELDS):
            for h in range(2):
                rows = slice(h * HALO, (h + 1) * HALO)
                own[f, i, rows, 0:LANES] = band[f, at, h]
                own[f, i, rows, LANES : 2 * LANES] = sides(f, at, h)

    odd = lax.rem(band_row, 2)
    for out, move in ((to_pair, 1 - 2 * odd), (to_other, 2 * odd - 1)):
        half = (move + 1) // 2
        other = lax.rem(band_row + move + band_rows, band_rows) * band_width
        packed = [None] * FIELDS
        for i in range(blocks):
            at = tropic[other + column * blocks + i] - other
            for f in range(FIELDS):
                out[f, i] = band[f, at, half]
                beside = sides(f, at, half)
                if i:
                    beside = pltpu.roll(beside, 2 * HALO * i, 1)
                packed[f] = beside if i == 0 else packed[f] + beside
        for f in range(FIELDS):
            out[f, blocks] = packed[f]


def select(spread, band_rows, parts, clinic, tropic, band_width, after):
    blocks, rows, lanes = parts[0].shape[1:]
    assert 2 * HALO * blocks <= LANES
    edge = jax.ShapeDtypeStruct((FIELDS, blocks + 1, HALO, lanes), F32)
    return pl.pallas_call(
        functools.partial(select_kernel, spread, band_rows),
        in_specs=[VMEM] * len(parts) + [SMEM] * 2 + [pl.BlockSpec(memory_space=pl.ANY)],
        out_specs=[VMEM] * 3,
        out_shape=[jax.ShapeDtypeStruct((FIELDS, blocks, rows, 2 * lanes), F32), edge, edge],
        scratch_shapes=[pltpu.VMEM((FIELDS, band_width, rows // HALO, HALO, lanes), F32)],
        compiler_params=params(16),
    )(*parts, clinic, tropic, after)


def two_sum(a, b):
    total = a + b
    part = total - a
    return total, (a - (total - part)) + (b - part)


def split(a):
    scaled = a * 4097.0
    high = scaled - (scaled - a)
    return high, a - high


def pair_add(a, b):
    high, low = two_sum(a[0], b[0])
    low = low + (a[1] + b[1])
    total = high + low
    return total, low - (total - high)


def product(a, b):
    value = a * b
    a_high, a_low = split(a)
    b_high, b_low = split(b)
    error = ((a_high * b_high - value) + a_high * b_low + a_low * b_high) + a_low * b_low
    return value, error


def fold(pair, axis, steps):
    for step in steps:
        pair = pair_add(pair, tuple(pltpu.roll(part, step, axis) for part in pair))
    return pair


def lane_sum(pair):
    high, low = pair
    grid = 384.0 * jnp.max(jnp.abs(high), axis=1, keepdims=True)
    lead = (high + grid) - grid
    rest = jnp.sum((high - lead) + low, axis=1, keepdims=True)
    return two_sum(jnp.sum(lead, axis=1, keepdims=True), rest)


def basis_kernel(levels, band_rows, own, from_pair, from_other, _, vectors, guess, sums, images):
    blocks, rows = own.shape[1], own.shape[2]
    tall = rows + 2 * HALO
    inner = slice(HALO, HALO + rows)
    lane = lax.broadcasted_iota(jnp.int32, (HALO, LANES), 1)
    beside = (lane < HALO) | (lane >= LANES - HALO)

    band_row = lax.axis_index("by")
    odd = lax.rem(band_row, 2) == 1

    def edge(from_odd, from_even, present, f, i):
        packed = jnp.where(odd, from_odd[f, blocks], from_even[f, blocks])
        if i:
            packed = pltpu.roll(packed, LANES - 2 * HALO * i, 1)
        middle = jnp.where(odd, from_odd[f, i], from_even[f, i])
        both = jnp.concatenate([middle, jnp.where(beside, packed, 0.0)], axis=1)
        return jnp.where(present, both, 0.0)

    def east(v):
        return pltpu.roll(v, 2 * LANES - 1, 1)

    def west(v):
        return pltpu.roll(v, 1, 1)

    def below(v):
        return pltpu.roll(v, tall - 1, 0)

    def above(v):
        return pltpu.roll(v, 1, 0)

    for i in range(blocks):
        forcing, depth, prior, ocean = (
            jnp.concatenate(
                [
                    edge(from_pair, from_other, band_row > 0, f, i),
                    own[f, i],
                    edge(from_other, from_pair, band_row < band_rows - 1, f, i),
                ],
                axis=0,
            )
            for f in range(FIELDS)
        )
        scale = FACE_SCALE / levels
        east_face = scale * jnp.minimum(depth, east(depth)) * ocean * east(ocean)
        south_face = scale * jnp.minimum(depth, below(depth)) * ocean * below(ocean)
        centre = SURFACE * ocean + (1.0 - ocean)
        diagonal = centre + east_face + west(east_face) + south_face + above(south_face)
        inverse = 1.0 / diagonal

        def operate(v):
            along = east_face * (v - east(v))
            across = south_face * (v - below(v))
            return centre * v + along - west(along) + across - above(across)

        first = ocean * prior
        residual = ocean * forcing - operate(first)
        v = residual * inverse
        guess[i] = first[inner, 0:LANES]
        place = slice(i * rows, (i + 1) * rows)
        images[ITERS, place] = residual[inner, 0:LANES]
        for k in range(ITERS):
            image = operate(v)
            vectors[k, place] = v[inner, 0:LANES]
            images[k, place] = image[inner, 0:LANES]
            if k + 1 < ITERS:
                following = image * inverse
                v = following - SHIFTS[k] * v if SHIFTS[k] else following

    row_id = lax.broadcasted_iota(jnp.int32, (8, LANES), 0)
    lane_id = lax.broadcasted_iota(jnp.int32, (8, LANES), 1)
    placed = None
    for begin in range(0, len(ENTRIES), 8):
        packed = (jnp.zeros((8, LANES), F32),) * 2
        for offset, (a, b) in enumerate(ENTRIES[begin : begin + 8]):
            total = error = None
            for r in range(0, blocks * rows, 8):
                value, rest = product(vectors[a, r : r + 8], images[b, r : r + 8])
                if total is None:
                    total, error = value, rest
                else:
                    total, extra = two_sum(total, value)
                    error = error + (rest + extra)
            pair = fold((total, error), 0, (4, 2, 1))
            packed = tuple(jnp.where(row_id == offset, new, old) for new, old in zip(pair, packed))
        high, low = lane_sum(packed)
        high = jnp.where(lane_id == row_id + begin, high, 0.0)
        low = jnp.where(lane_id == row_id + (begin + LANES // 2), low, 0.0)
        placed = high + low if placed is None else placed + high + low
    for step in (4, 2, 1):
        placed = placed + pltpu.roll(placed, step, 0)
    sums[...] = jnp.broadcast_to(placed[0:1][None], sums.shape)


def basis(levels, own, from_pair, from_other, after, band_rows, devices):
    fields, blocks, rows, _ = own.shape
    return pl.pallas_call(
        functools.partial(basis_kernel, levels, band_rows),
        in_specs=[VMEM] * 3 + [pl.BlockSpec(memory_space=pl.ANY)],
        out_specs=[VMEM] * 3,
        out_shape=[
            jax.ShapeDtypeStruct((ITERS, blocks * rows, LANES), F32),
            jax.ShapeDtypeStruct((blocks, rows, LANES), F32),
            jax.ShapeDtypeStruct((devices, 1, LANES), F32),
        ],
        scratch_shapes=[pltpu.VMEM((ITERS + 1, blocks * rows, LANES), F32)],
        compiler_params=params(16),
    )(own, from_pair, from_other, after)


def finish_kernel(sums, vectors, guess, out):
    devices = sums.shape[0]
    blocks, rows = guess.shape[0], guess.shape[1]
    pairs = [(sums[d : d + 8], jnp.zeros((8, LANES), F32)) for d in range(0, devices, 8)]
    while len(pairs) > 1:
        pairs = [pair_add(pairs[j], pairs[j + 1]) for j in range(0, len(pairs), 2)]
    total, error = fold(pairs[0], 0, (4, 2, 1))
    low = error + pltpu.roll(total, 64, 1)
    entry = {
        pair: tuple(jnp.broadcast_to(part[:, n : n + 1], (8, LANES)) for part in (total, low))
        for n, pair in enumerate(ENTRIES)
    }
    energy = [entry[k, k][0] for k in range(ITERS)]
    inverse, below = [], {}
    for k in range(ITERS):
        pivot = entry[k, k]
        good = pivot[0] > PIVOT_FLOOR * energy[k]
        inverse.append(jnp.where(good, 1.0 / jnp.where(good, pivot[0], 1.0), 0.0))
        for i in range(k + 1, ITERS):
            side = entry[k, i]
            lead = side[0] * inverse[k]
            value, error = product(lead, pivot[0])
            rest = ((side[0] - value) - error) + (side[1] - lead * pivot[1])
            below[i, k] = (lead, rest * inverse[k])
        for i in range(k + 1, ITERS):
            lead, rest = below[i, k]
            for j in range(i, ITERS + 1):
                across = entry[k, j]
                value, error = product(lead, across[0])
                error = error + (lead * across[1] + rest * across[0])
                entry[i, j] = pair_add(entry[i, j], (-value, -error))
    weights = [entry[k, ITERS][0] * inverse[k] for k in range(ITERS)]
    for k in range(ITERS - 2, -1, -1):
        for i in range(ITERS - 1, k, -1):
            weights[k] = weights[k] - below[i, k][0] * weights[i]
    for b in range(blocks):
        for r in range(0, rows, 8):
            at = b * rows + r
            result = guess[b, r : r + 8]
            for k in range(ITERS):
                result = result + weights[k] * vectors[k, at : at + 8]
            out[b, r : r + 8] = result


def finish(sums, vectors, guess):
    return pl.pallas_call(
        finish_kernel,
        in_specs=[VMEM] * 3,
        out_specs=VMEM,
        out_shape=jax.ShapeDtypeStruct(guess.shape, F32),
        compiler_params=params(16),
    )(sums, vectors, guess)


def swap(array, axis, hop):
    count = lax.axis_size(axis)
    return lax.ppermute(array, axis, [(i, i ^ hop) for i in range(count)])


def other_partners(band_rows, holders):
    pairs = []
    for row in range(band_rows):
        other = ((row + 1) ^ 1) - 1
        for column in range(holders):
            inside = 0 <= other < band_rows
            target = (other, column) if inside else (row, column ^ 1)
            pairs.append((row * holders + column, target[0] * holders + target[1]))
    return pairs


def local(
    tracers,
    vertical_speed,
    diffusivity,
    buoyancy_force,
    wet_levels,
    surface_patch,
    prior_height,
    land_mask,
    baroclinic_map,
    barotropic_map,
):
    levels, blocks, _, cells = tracers.shape
    band_rows, holders = lax.axis_size("by"), lax.axis_size("bx")
    early = cells // CHUNK * blocks * EARLY // 16

    payload, clinic, tropic = payload_of(
        buoyancy_force, wet_levels, prior_height, land_mask, baroclinic_map, barotropic_map
    )
    spread = list(range(0, holders, 2))
    parts = [payload] + [swap(payload, "bx", hop) for hop in spread[1:]]
    stepped, mark, regions, *factors = first_columns(
        tracers, vertical_speed, diffusivity, wet_levels, surface_patch, early, payload
    )
    *parts, mark = lax.optimization_barrier((*parts, mark))
    parts = parts + [swap(part, "bx", 1) for part in parts]
    spread = spread + [hop + 1 for hop in spread]

    own, to_pair, to_other = select(
        tuple(spread), band_rows, parts, clinic, tropic, holders * blocks, mark
    )
    from_pair = swap(to_pair, "by", 1)
    from_other = lax.ppermute(to_other, ("by", "bx"), other_partners(band_rows, holders))
    stepped, late = rest_columns(tracers, early, stepped, regions, factors, to_other)
    from_pair, from_other, late = lax.optimization_barrier((from_pair, from_other, late))
    vectors, guess, sums = basis(
        levels, own, from_pair, from_other, late, band_rows, band_rows * holders
    )
    gathered = lax.all_to_all(sums, ("by", "bx"), 0, 0, tiled=True)
    gathered = gathered.reshape(band_rows * holders, LANES)
    return stepped, finish(gathered, vectors, guess)


def solution(mesh):
    slots = ("by", "bx")
    return jax.shard_map(
        local,
        mesh=mesh,
        in_specs=(
            P(None, slots, None, None),
            P(None, slots, None),
            P(None, slots, None),
            P(None, slots, None),
            P(slots, None),
            P(slots, None),
            P(slots, None),
            P(slots, None, None),
            P(),
            P(),
        ),
        out_specs=(P(None, slots, None, None), P(slots, None, None)),
        check_vma=False,
    )
```

```python
import functools

import jax
import jax.numpy as jnp
from jax import lax
from jax.experimental import pallas as pl
from jax.experimental.pallas import tpu as pltpu
from jax.sharding import PartitionSpec as P

ITERS = 6
RESTORE = 0.5
SURFACE = 0.1
FACE_SCALE = 2.0
PIVOT_FLOOR = 1e-11
HALO = 8
LANES = 128
FIELDS = 4
ENTRIES = [(a, b) for a in range(ITERS) for b in range(a, ITERS + 1)]
CHUNK = 512
EARLY = 9
F32 = jnp.float32
VMEM = pl.BlockSpec(memory_space=pltpu.VMEM)
SMEM = pl.BlockSpec(memory_space=pltpu.SMEM)
HBM = pl.BlockSpec(memory_space=pltpu.HBM)


def in_hbm(*arrays):
    return [pltpu.with_memory_space_constraint(array, pltpu.HBM) for array in arrays]


def params(mebibytes):
    return pltpu.CompilerParams(vmem_limit_bytes=mebibytes * 2**20)


def fold_columns(speed, mixing, wet, patch, regions, factors):
    enter, keep, raise_, lower, sink = factors
    levels = speed.shape[0]
    tiles = speed.shape[2] // LANES

    def stacked(block):
        return jnp.concatenate([block[:, t * LANES : (t + 1) * LANES] for t in range(tiles)], axis=0)

    regions[...] = stacked(patch[...])
    wet_now = stacked(wet[...])
    zero = jnp.zeros(wet_now.shape, F32)
    mix_above, up_above, down_above, inverse = zero, zero, zero, zero
    for k in range(levels):
        is_wet = (k < wet_now).astype(F32)
        is_open = (k + 1 < wet_now).astype(F32)
        flow = stacked(speed[k]) * is_open
        up, down = jnp.maximum(flow, 0.0), jnp.minimum(flow, 0.0)
        mix = stacked(mixing[k]) * is_open
        diagonal = 1.0 + mix + mix_above
        if k == 0:
            source = RESTORE * is_wet
            diagonal = diagonal + source
        inverse = 1.0 / (diagonal - mix_above * (mix_above * inverse))
        scaled_wet = is_wet * inverse
        keep[k] = scaled_wet * (1.0 + down - up_above)
        raise_[k] = scaled_wet * up
        lower[k] = mix * inverse
        enter[k] = (source if k == 0 else mix_above) * inverse
        sink[k] = scaled_wet * down_above
        mix_above, up_above, down_above = mix, up, down


def sweep(begin, tracers, out, regions, factors, held, in_sems, out_sems):
    enter, keep, raise_, lower, sink = factors
    steps, levels, count, width = held.shape
    blocks = tracers.shape[1]
    tiles = width // LANES

    def place(ref, j):
        slot = lax.rem(j + begin, blocks)
        at = pl.multiple_of((j + begin) // blocks * width, width)
        return ref.at[:, slot, :, pl.ds(at, width)]

    def load(j):
        return pltpu.make_async_copy(place(tracers, j), held.at[j], in_sems.at[j])

    def store(j):
        return pltpu.make_async_copy(held.at[j], place(out, j), out_sems.at[j])

    tracer_ids = lax.broadcasted_iota(jnp.int32, (count, width), 0)

    def solve(j, carry):
        load(j).wait()
        slot = lax.rem(j + begin, blocks)
        first = (j + begin) // blocks * tiles

        def rows(take):
            return jnp.concatenate(
                [
                    jnp.broadcast_to(take(pl.ds((first + t) * blocks + slot, 1)), (count, LANES))
                    for t in range(tiles)
                ],
                axis=1,
            )

        def row(ref, k):
            return rows(lambda at: ref[k, at, :])

        above = value = None
        here = held[j, 0]
        for k in range(levels):
            result = row(keep, k) * here
            if k + 1 < levels:
                below = held[j, k + 1]
                result = result + row(raise_, k) * below
            if k == 0:
                target = (rows(lambda at: regions[at, :]) == tracer_ids).astype(F32)
                result = result + row(enter, k) * target
            else:
                result = result - row(sink, k) * above
                result = result + row(enter, k) * value
            value = result
            held[j, k] = value
            if k + 1 < levels:
                above, here = here, below
        for k in range(levels - 2, -1, -1):
            value = held[j, k] + row(lower, k) * value
            held[j, k] = value
        store(j).start()
        return carry

    def run(prepare):
        for j in range(steps):
            load(j).start()
        prepare()
        lax.fori_loop(0, steps, solve, 0)
        for j in range(steps):
            store(j).wait()

    return run


def first_columns_kernel(tracers, speed, mixing, wet, patch, after, out, mark, regions, *rest):
    factors, (held, speed_in, mixing_in, wet_in, patch_in, sems, in_sems, out_sems) = rest[:5], rest[5:]
    copies = [
        pltpu.make_async_copy(source, target, sems.at[j])
        for j, (source, target) in enumerate(
            ((speed, speed_in), (mixing, mixing_in), (wet, wet_in), (patch, patch_in))
        )
    ]
    for copy in copies:
        copy.start()

    def prepare():
        for copy in copies:
            copy.wait()
        fold_columns(speed_in, mixing_in, wet_in, patch_in, regions, factors)

    mark[...] = jnp.zeros(mark.shape, F32)
    sweep(0, tracers, out, regions, factors, held, in_sems, out_sems)(prepare)


def first_columns(tracers, speed, mixing, wet, patch, steps, after):
    levels, blocks, count, cells = tracers.shape
    rows = cells // LANES * blocks
    factor = jax.ShapeDtypeStruct((levels, rows, LANES), F32)
    return pl.pallas_call(
        first_columns_kernel,
        in_specs=[HBM] * 5 + [pl.BlockSpec(memory_space=pl.ANY)],
        out_specs=[HBM] + [VMEM] * 7,
        out_shape=[
            jax.ShapeDtypeStruct(tracers.shape, F32),
            jax.ShapeDtypeStruct((8, LANES), F32),
            jax.ShapeDtypeStruct((rows, LANES), jnp.int32),
        ]
        + [factor] * 5,
        scratch_shapes=[pltpu.VMEM((steps, levels, count, CHUNK), F32)]
        + [pltpu.VMEM(each.shape, each.dtype) for each in (speed, mixing, wet, patch)]
        + [pltpu.SemaphoreType.DMA((n,)) for n in (4, steps, steps)],
        compiler_params=params(40),
        cost_estimate=column_cost(tracers, steps),
    )(*in_hbm(tracers, speed, mixing, wet, patch), after)


def rest_columns_kernel(begin, tracers, regions, *rest):
    factors, (_, _, out, mark, held, in_sems, out_sems) = rest[:5], rest[5:]
    mark[...] = jnp.zeros(mark.shape, F32)
    sweep(begin, tracers, out, regions, factors, held, in_sems, out_sems)(lambda: None)


def rest_columns(tracers, begin, previous, regions, factors, after):
    levels, blocks, count, cells = tracers.shape
    steps = cells // CHUNK * blocks - begin
    return pl.pallas_call(
        functools.partial(rest_columns_kernel, begin),
        in_specs=[HBM] + [VMEM] * 6 + [HBM, pl.BlockSpec(memory_space=pl.ANY)],
        out_specs=[HBM, VMEM],
        out_shape=[
            jax.ShapeDtypeStruct(tracers.shape, F32),
            jax.ShapeDtypeStruct((8, LANES), F32),
        ],
        scratch_shapes=[pltpu.VMEM((steps, levels, count, CHUNK), F32)]
        + [pltpu.SemaphoreType.DMA((steps,))] * 2,
        input_output_aliases={7: 0},
        compiler_params=params(24),
        cost_estimate=column_cost(tracers, steps),
    )(*in_hbm(tracers), regions, *factors, *in_hbm(previous), after)


def column_cost(tracers, steps):
    levels, _, count, _ = tracers.shape
    part = steps * CHUNK * levels
    return pl.CostEstimate(
        flops=part * count * 10, bytes_accessed=part * (count * 8 + 8), transcendentals=0
    )


def payload_kernel(buoyancy, wet, prior, land, clinic, tropic, out, clinic_out, tropic_out, force, wet_in, prior_in, land_in, sems):
    copies = [
        pltpu.make_async_copy(source, target, sems.at[j])
        for j, (source, target) in enumerate(
            (
                (buoyancy, force),
                (wet, wet_in),
                (prior, prior_in),
                (land, land_in),
                (clinic, clinic_out),
                (tropic, tropic_out),
            )
        )
    ]
    for copy in copies:
        copy.start()
    for copy in copies:
        copy.wait()
    levels, blocks, cells = force.shape
    rows = cells // LANES
    wet_now = wet_in[...]
    total = jnp.zeros(wet_now.shape, F32)
    for k in range(levels):
        total = total + (k < wet_now).astype(F32) * force[k].astype(F32)
    depth = wet_now.astype(F32)
    first = prior_in[...]
    for r in range(rows):
        lanes = slice(r * LANES, (r + 1) * LANES)
        out[0, :, r, :] = total[:, lanes]
        out[1, :, r, :] = depth[:, lanes]
        out[2, :, r, :] = first[:, lanes]
    out[3] = land_in[...].astype(F32)


def payload_of(buoyancy, wet, prior, land, clinic, tropic):
    blocks, rows, lanes = land.shape
    return pl.pallas_call(
        payload_kernel,
        in_specs=[HBM] * 6,
        out_specs=[VMEM] * 3,
        out_shape=[
            jax.ShapeDtypeStruct((FIELDS, blocks, rows, lanes), F32),
            jax.ShapeDtypeStruct(clinic.shape, clinic.dtype),
            jax.ShapeDtypeStruct(tropic.shape, tropic.dtype),
        ],
        scratch_shapes=[
            pltpu.VMEM(each.shape, each.dtype) for each in (buoyancy, wet, prior, land)
        ]
        + [pltpu.SemaphoreType.DMA((6,))],
        compiler_params=params(16),
    )(*in_hbm(buoyancy, wet, prior, land, clinic, tropic))


def select_kernel(spread, band_rows, *refs):
    parts = refs[: len(spread)]
    clinic, tropic, _, own, to_pair, to_other, band = refs[len(spread) :]
    blocks = own.shape[1]
    band_width = band.shape[1]
    band_row, column = lax.axis_index("by"), lax.axis_index("bx")
    first_slot = band_row * band_width
    for hop, ref in zip(spread, parts):
        holder = (column ^ hop) * blocks
        for s in range(blocks):
            slot = first_slot + holder + s
            at = clinic[slot] - first_slot
            for f in range(FIELDS - 1):
                for h in range(2):
                    band[f, at, h] = ref[f, s, h * HALO : (h + 1) * HALO]
            at = tropic[slot] - first_slot
            for h in range(2):
                band[FIELDS - 1, at, h] = ref[FIELDS - 1, s, h * HALO : (h + 1) * HALO]

    lane = lax.broadcasted_iota(jnp.int32, (HALO, LANES), 1)

    def sides(f, at, half):
        east = lax.rem(at + 1, band_width)
        west = lax.rem(at + band_width - 1, band_width)
        return jnp.where(
            lane < HALO,
            band[f, east, half],
            jnp.where(lane >= LANES - HALO, band[f, west, half], 0.0),
        )

    for i in range(blocks):
        at = tropic[first_slot + column * blocks + i] - first_slot
        for f in range(FIELDS):
            for h in range(2):
                rows = slice(h * HALO, (h + 1) * HALO)
                own[f, i, rows, 0:LANES] = band[f, at, h]
                own[f, i, rows, LANES : 2 * LANES] = sides(f, at, h)

    odd = lax.rem(band_row, 2)
    for out, move in ((to_pair, 1 - 2 * odd), (to_other, 2 * odd - 1)):
        half = (move + 1) // 2
        other = lax.rem(band_row + move + band_rows, band_rows) * band_width
        packed = [None] * FIELDS
        for i in range(blocks):
            at = tropic[other + column * blocks + i] - other
            for f in range(FIELDS):
                out[f, i] = band[f, at, half]
                beside = sides(f, at, half)
                if i:
                    beside = pltpu.roll(beside, 2 * HALO * i, 1)
                packed[f] = beside if i == 0 else packed[f] + beside
        for f in range(FIELDS):
            out[f, blocks] = packed[f]


def select(spread, band_rows, parts, clinic, tropic, band_width, after):
    blocks, rows, lanes = parts[0].shape[1:]
    assert 2 * HALO * blocks <= LANES
    edge = jax.ShapeDtypeStruct((FIELDS, blocks + 1, HALO, lanes), F32)
    return pl.pallas_call(
        functools.partial(select_kernel, spread, band_rows),
        in_specs=[VMEM] * len(parts) + [SMEM] * 2 + [pl.BlockSpec(memory_space=pl.ANY)],
        out_specs=[VMEM] * 3,
        out_shape=[jax.ShapeDtypeStruct((FIELDS, blocks, rows, 2 * lanes), F32), edge, edge],
        scratch_shapes=[pltpu.VMEM((FIELDS, band_width, rows // HALO, HALO, lanes), F32)],
        compiler_params=params(16),
    )(*parts, clinic, tropic, after)


def two_sum(a, b):
    total = a + b
    part = total - a
    return total, (a - (total - part)) + (b - part)


def split(a):
    scaled = a * 4097.0
    high = scaled - (scaled - a)
    return high, a - high


def pair_add(a, b):
    high, low = two_sum(a[0], b[0])
    low = low + (a[1] + b[1])
    total = high + low
    return total, low - (total - high)


def product(a, b):
    value = a * b
    a_high, a_low = split(a)
    b_high, b_low = split(b)
    error = ((a_high * b_high - value) + a_high * b_low + a_low * b_high) + a_low * b_low
    return value, error


def fold(pair, axis, steps):
    for step in steps:
        pair = pair_add(pair, tuple(pltpu.roll(part, step, axis) for part in pair))
    return pair


def lane_sum(pair):
    high, low = pair
    grid = 384.0 * jnp.max(jnp.abs(high), axis=1, keepdims=True)
    lead = (high + grid) - grid
    rest = jnp.sum((high - lead) + low, axis=1, keepdims=True)
    return two_sum(jnp.sum(lead, axis=1, keepdims=True), rest)


def basis_kernel(levels, band_rows, own, from_pair, from_other, _, vectors, guess, sums, images):
    blocks, rows = own.shape[1], own.shape[2]
    tall = rows + 2 * HALO
    inner = slice(HALO, HALO + rows)
    lane = lax.broadcasted_iota(jnp.int32, (HALO, LANES), 1)
    beside = (lane < HALO) | (lane >= LANES - HALO)

    band_row = lax.axis_index("by")
    odd = lax.rem(band_row, 2) == 1

    def edge(from_odd, from_even, present, f, i):
        packed = jnp.where(odd, from_odd[f, blocks], from_even[f, blocks])
        if i:
            packed = pltpu.roll(packed, LANES - 2 * HALO * i, 1)
        middle = jnp.where(odd, from_odd[f, i], from_even[f, i])
        both = jnp.concatenate([middle, jnp.where(beside, packed, 0.0)], axis=1)
        return jnp.where(present, both, 0.0)

    def east(v):
        return pltpu.roll(v, 2 * LANES - 1, 1)

    def west(v):
        return pltpu.roll(v, 1, 1)

    def below(v):
        return pltpu.roll(v, tall - 1, 0)

    def above(v):
        return pltpu.roll(v, 1, 0)

    for i in range(blocks):
        forcing, depth, prior, ocean = (
            jnp.concatenate(
                [
                    edge(from_pair, from_other, band_row > 0, f, i),
                    own[f, i],
                    edge(from_other, from_pair, band_row < band_rows - 1, f, i),
                ],
                axis=0,
            )
            for f in range(FIELDS)
        )
        scale = FACE_SCALE / levels
        east_face = scale * jnp.minimum(depth, east(depth)) * ocean * east(ocean)
        south_face = scale * jnp.minimum(depth, below(depth)) * ocean * below(ocean)
        centre = SURFACE * ocean + (1.0 - ocean)
        diagonal = centre + east_face + west(east_face) + south_face + above(south_face)
        inverse = 1.0 / diagonal

        def operate(v):
            along = east_face * (v - east(v))
            across = south_face * (v - below(v))
            return centre * v + along - west(along) + across - above(across)

        first = ocean * prior
        residual = ocean * forcing - operate(first)
        v = residual * inverse
        guess[i] = first[inner, 0:LANES]
        place = slice(i * rows, (i + 1) * rows)
        images[ITERS, place] = residual[inner, 0:LANES]
        for k in range(ITERS):
            image = operate(v)
            vectors[k, place] = v[inner, 0:LANES]
            images[k, place] = image[inner, 0:LANES]
            if k + 1 < ITERS:
                following = image * inverse
                if k == 1:
                    following = v - following
                elif k > 1:
                    following = 2.0 * (v - following) - before
                before, v = v, following

    row_id = lax.broadcasted_iota(jnp.int32, (8, LANES), 0)
    lane_id = lax.broadcasted_iota(jnp.int32, (8, LANES), 1)
    placed = None
    for begin in range(0, len(ENTRIES), 8):
        packed = (jnp.zeros((8, LANES), F32),) * 2
        for offset, (a, b) in enumerate(ENTRIES[begin : begin + 8]):
            total = error = None
            for r in range(0, blocks * rows, 8):
                value, rest = product(vectors[a, r : r + 8], images[b, r : r + 8])
                if total is None:
                    total, error = value, rest
                else:
                    total, extra = two_sum(total, value)
                    error = error + (rest + extra)
            pair = fold((total, error), 0, (4, 2, 1))
            packed = tuple(jnp.where(row_id == offset, new, old) for new, old in zip(pair, packed))
        high, low = lane_sum(packed)
        high = jnp.where(lane_id == row_id + begin, high, 0.0)
        low = jnp.where(lane_id == row_id + (begin + LANES // 2), low, 0.0)
        placed = high + low if placed is None else placed + high + low
    for step in (4, 2, 1):
        placed = placed + pltpu.roll(placed, step, 0)
    sums[...] = jnp.broadcast_to(placed[0:1][None], sums.shape)


def basis(levels, own, from_pair, from_other, after, band_rows, devices):
    fields, blocks, rows, _ = own.shape
    return pl.pallas_call(
        functools.partial(basis_kernel, levels, band_rows),
        in_specs=[VMEM] * 3 + [pl.BlockSpec(memory_space=pl.ANY)],
        out_specs=[VMEM] * 3,
        out_shape=[
            jax.ShapeDtypeStruct((ITERS, blocks * rows, LANES), F32),
            jax.ShapeDtypeStruct((blocks, rows, LANES), F32),
            jax.ShapeDtypeStruct((devices, 1, LANES), F32),
        ],
        scratch_shapes=[pltpu.VMEM((ITERS + 1, blocks * rows, LANES), F32)],
        compiler_params=params(16),
    )(own, from_pair, from_other, after)


def finish_kernel(sums, vectors, guess, out):
    devices = sums.shape[0]
    blocks, rows = guess.shape[0], guess.shape[1]
    pairs = [(sums[d : d + 8], jnp.zeros((8, LANES), F32)) for d in range(0, devices, 8)]
    while len(pairs) > 1:
        pairs = [pair_add(pairs[j], pairs[j + 1]) for j in range(0, len(pairs), 2)]
    total, error = fold(pairs[0], 0, (4, 2, 1))
    low = error + pltpu.roll(total, 64, 1)
    entry = {
        pair: tuple(jnp.broadcast_to(part[:, n : n + 1], (8, LANES)) for part in (total, low))
        for n, pair in enumerate(ENTRIES)
    }
    energy = [entry[k, k][0] for k in range(ITERS)]
    inverse, below = [], {}
    for k in range(ITERS):
        pivot = entry[k, k]
        good = pivot[0] > PIVOT_FLOOR * energy[k]
        inverse.append(jnp.where(good, 1.0 / jnp.where(good, pivot[0], 1.0), 0.0))
        for i in range(k + 1, ITERS):
            side = entry[k, i]
            lead = side[0] * inverse[k]
            value, error = product(lead, pivot[0])
            rest = ((side[0] - value) - error) + (side[1] - lead * pivot[1])
            below[i, k] = (lead, rest * inverse[k])
        for i in range(k + 1, ITERS):
            lead, rest = below[i, k]
            for j in range(i, ITERS + 1):
                across = entry[k, j]
                value, error = product(lead, across[0])
                error = error + (lead * across[1] + rest * across[0])
                entry[i, j] = pair_add(entry[i, j], (-value, -error))
    weights = [entry[k, ITERS][0] * inverse[k] for k in range(ITERS)]
    for k in range(ITERS - 2, -1, -1):
        for i in range(ITERS - 1, k, -1):
            weights[k] = weights[k] - below[i, k][0] * weights[i]
    for b in range(blocks):
        for r in range(0, rows, 8):
            at = b * rows + r
            result = guess[b, r : r + 8]
            for k in range(ITERS):
                result = result + weights[k] * vectors[k, at : at + 8]
            out[b, r : r + 8] = result


def finish(sums, vectors, guess):
    return pl.pallas_call(
        finish_kernel,
        in_specs=[VMEM] * 3,
        out_specs=VMEM,
        out_shape=jax.ShapeDtypeStruct(guess.shape, F32),
        compiler_params=params(16),
    )(sums, vectors, guess)


def swap(array, axis, hop):
    count = lax.axis_size(axis)
    return lax.ppermute(array, axis, [(i, i ^ hop) for i in range(count)])


def other_partners(band_rows, holders):
    pairs = []
    for row in range(band_rows):
        other = ((row + 1) ^ 1) - 1
        for column in range(holders):
            inside = 0 <= other < band_rows
            target = (other, column) if inside else (row, column ^ 1)
            pairs.append((row * holders + column, target[0] * holders + target[1]))
    return pairs


def local(
    tracers,
    vertical_speed,
    diffusivity,
    buoyancy_force,
    wet_levels,
    surface_patch,
    prior_height,
    land_mask,
    baroclinic_map,
    barotropic_map,
):
    levels, blocks, _, cells = tracers.shape
    band_rows, holders = lax.axis_size("by"), lax.axis_size("bx")
    early = cells // CHUNK * blocks * EARLY // 16

    payload, clinic, tropic = payload_of(
        buoyancy_force, wet_levels, prior_height, land_mask, baroclinic_map, barotropic_map
    )
    spread = list(range(0, holders, 2))
    parts = [payload] + [swap(payload, "bx", hop) for hop in spread[1:]]
    stepped, mark, regions, *factors = first_columns(
        tracers, vertical_speed, diffusivity, wet_levels, surface_patch, early, payload
    )
    beside = swap(payload, "bx", 1)
    beside, *parts, mark = lax.optimization_barrier((beside, *parts, mark))
    parts = parts + [beside] + [swap(part, "bx", 1) for part in parts[1:]]
    spread = spread + [hop + 1 for hop in spread]

    own, to_pair, to_other = select(
        tuple(spread), band_rows, parts, clinic, tropic, holders * blocks, mark
    )
    from_pair = swap(to_pair, "by", 1)
    from_other = lax.ppermute(to_other, ("by", "bx"), other_partners(band_rows, holders))
    stepped, late = rest_columns(tracers, early, stepped, regions, factors, to_other)
    from_pair, from_other, late = lax.optimization_barrier((from_pair, from_other, late))
    vectors, guess, sums = basis(
        levels, own, from_pair, from_other, late, band_rows, band_rows * holders
    )
    gathered = lax.all_to_all(sums, ("by", "bx"), 0, 0, tiled=True)
    gathered = gathered.reshape(band_rows * holders, LANES)
    return stepped, finish(gathered, vectors, guess)


def solution(mesh):
    slots = ("by", "bx")
    return jax.shard_map(
        local,
        mesh=mesh,
        in_specs=(
            P(None, slots, None, None),
            P(None, slots, None),
            P(None, slots, None),
            P(None, slots, None),
            P(slots, None),
            P(slots, None),
            P(slots, None),
            P(slots, None, None),
            P(),
            P(),
        ),
        out_specs=(P(None, slots, None, None), P(slots, None, None)),
        check_vma=False,
    )
```

```python
import functools

import jax
import jax.numpy as jnp
from jax import lax
from jax.experimental import pallas as pl
from jax.experimental.pallas import tpu as pltpu
from jax.sharding import PartitionSpec as P

ITERS = 6
RESTORE = 0.5
SURFACE = 0.1
FACE_SCALE = 2.0
PIVOT_FLOOR = 1e-11
HALO = 8
LANES = 128
FIELDS = 4
ENTRIES = [(a, b) for a in range(ITERS) for b in range(a, ITERS + 1)]
CHUNK = 512
EARLY = 7
F32 = jnp.float32
VMEM = pl.BlockSpec(memory_space=pltpu.VMEM)
SMEM = pl.BlockSpec(memory_space=pltpu.SMEM)
HBM = pl.BlockSpec(memory_space=pltpu.HBM)


def in_hbm(*arrays):
    return [pltpu.with_memory_space_constraint(array, pltpu.HBM) for array in arrays]


def params(mebibytes):
    return pltpu.CompilerParams(vmem_limit_bytes=mebibytes * 2**20)


def fold_columns(speed, mixing, wet, patch, regions, factors):
    enter, keep, raise_, lower, sink = factors
    levels = speed.shape[0]
    tiles = speed.shape[2] // LANES

    def stacked(block):
        return jnp.concatenate([block[:, t * LANES : (t + 1) * LANES] for t in range(tiles)], axis=0)

    regions[...] = stacked(patch[...])
    wet_now = stacked(wet[...])
    zero = jnp.zeros(wet_now.shape, F32)
    mix_above, up_above, down_above, inverse = zero, zero, zero, zero
    for k in range(levels):
        is_wet = (k < wet_now).astype(F32)
        is_open = (k + 1 < wet_now).astype(F32)
        flow = stacked(speed[k]) * is_open
        up, down = jnp.maximum(flow, 0.0), jnp.minimum(flow, 0.0)
        mix = stacked(mixing[k]) * is_open
        diagonal = 1.0 + mix + mix_above
        if k == 0:
            source = RESTORE * is_wet
            diagonal = diagonal + source
        inverse = 1.0 / (diagonal - mix_above * (mix_above * inverse))
        scaled_wet = is_wet * inverse
        keep[k] = scaled_wet * (1.0 + down - up_above)
        raise_[k] = scaled_wet * up
        lower[k] = mix * inverse
        enter[k] = (source if k == 0 else mix_above) * inverse
        sink[k] = scaled_wet * down_above
        mix_above, up_above, down_above = mix, up, down


def sweep(begin, tracers, out, regions, factors, held, in_sems, out_sems, ready=None):
    enter, keep, raise_, lower, sink = factors
    steps, levels, count, width = held.shape
    blocks = out.shape[1]
    tiles = width // LANES

    def place(ref, j):
        slot = lax.rem(j + begin, blocks)
        at = pl.multiple_of((j + begin) // blocks * width, width)
        return ref.at[:, slot, :, pl.ds(at, width)]

    def load(j):
        return pltpu.make_async_copy(place(tracers, j), held.at[j], in_sems.at[j])

    def store(j):
        return pltpu.make_async_copy(held.at[j], place(out, j), out_sems.at[j])

    tracer_ids = lax.broadcasted_iota(jnp.int32, (count, width), 0)

    def solve(j, carry):
        if ready is None:
            load(j).wait()
        slot = lax.rem(j + begin, blocks)
        first = (j + begin) // blocks * tiles

        def rows(take):
            return jnp.concatenate(
                [
                    jnp.broadcast_to(take(pl.ds((first + t) * blocks + slot, 1)), (count, LANES))
                    for t in range(tiles)
                ],
                axis=1,
            )

        def row(ref, k):
            return rows(lambda at: ref[k, at, :])

        above = value = None
        def given(k):
            if ready is None:
                return held[j, k]
            at = pl.multiple_of((j + begin) // blocks * width, width)
            return ready[k, slot, :, pl.ds(at, width)]

        here = given(0)
        for k in range(levels):
            result = row(keep, k) * here
            if k + 1 < levels:
                below = given(k + 1)
                result = result + row(raise_, k) * below
            if k == 0:
                target = (rows(lambda at: regions[at, :]) == tracer_ids).astype(F32)
                result = result + row(enter, k) * target
            else:
                result = result - row(sink, k) * above
                result = result + row(enter, k) * value
            value = result
            held[j, k] = value
            if k + 1 < levels:
                above, here = here, below
        for k in range(levels - 2, -1, -1):
            value = held[j, k] + row(lower, k) * value
            held[j, k] = value
        store(j).start()
        return carry

    def run(prepare):
        for j in range(steps if ready is None else 0):
            load(j).start()
        prepare()
        lax.fori_loop(0, steps, solve, 0)
        for j in range(steps):
            store(j).wait()

    return run


def first_columns_kernel(tracers, speed, mixing, wet, patch, after, out, mark, regions, *rest):
    factors, (held, speed_in, mixing_in, wet_in, patch_in, sems, in_sems, out_sems) = rest[:5], rest[5:]
    copies = [
        pltpu.make_async_copy(source, target, sems.at[j])
        for j, (source, target) in enumerate(
            ((speed, speed_in), (mixing, mixing_in), (wet, wet_in), (patch, patch_in))
        )
    ]
    for copy in copies:
        copy.start()

    def prepare():
        for copy in copies:
            copy.wait()
        fold_columns(speed_in, mixing_in, wet_in, patch_in, regions, factors)

    mark[...] = jnp.zeros(mark.shape, F32)
    sweep(0, tracers, out, regions, factors, held, in_sems, out_sems)(prepare)


def first_columns(tracers, speed, mixing, wet, patch, steps, after):
    levels, blocks, count, cells = tracers.shape
    rows = cells // LANES * blocks
    factor = jax.ShapeDtypeStruct((levels, rows, LANES), F32)
    return pl.pallas_call(
        first_columns_kernel,
        in_specs=[HBM] * 5 + [pl.BlockSpec(memory_space=pl.ANY)],
        out_specs=[HBM] + [VMEM] * 7,
        out_shape=[
            jax.ShapeDtypeStruct(tracers.shape, F32),
            jax.ShapeDtypeStruct((8, LANES), F32),
            jax.ShapeDtypeStruct((rows, LANES), jnp.int32),
        ]
        + [factor] * 5,
        scratch_shapes=[pltpu.VMEM((steps, levels, count, CHUNK), F32)]
        + [pltpu.VMEM(each.shape, each.dtype) for each in (speed, mixing, wet, patch)]
        + [pltpu.SemaphoreType.DMA((n,)) for n in (4, steps, steps)],
        compiler_params=params(40),
        cost_estimate=column_cost(tracers, steps),
    )(*in_hbm(tracers, speed, mixing, wet, patch), after)


def rest_columns_kernel(begin, tracers, regions, *rest):
    factors, (_, _, out, mark, held, in_sems, out_sems) = rest[:5], rest[5:]
    mark[...] = jnp.zeros(mark.shape, F32)
    sweep(begin, None, out, regions, factors, held, in_sems, out_sems, tracers)(lambda: None)


def rest_columns(tracers, begin, previous, regions, factors, after):
    levels, blocks, count, cells = tracers.shape
    steps = cells // CHUNK * blocks - begin
    return pl.pallas_call(
        functools.partial(rest_columns_kernel, begin),
        in_specs=[VMEM] * 7 + [HBM, pl.BlockSpec(memory_space=pl.ANY)],
        out_specs=[HBM, VMEM],
        out_shape=[
            jax.ShapeDtypeStruct(previous.shape, F32),
            jax.ShapeDtypeStruct((8, LANES), F32),
        ],
        scratch_shapes=[pltpu.VMEM((steps, levels, count, CHUNK), F32)]
        + [pltpu.SemaphoreType.DMA((steps,))] * 2,
        input_output_aliases={7: 0},
        compiler_params=params(24),
        cost_estimate=column_cost(tracers, steps),
    )(tracers, regions, *factors, *in_hbm(previous), after)


def column_cost(tracers, steps):
    levels, _, count, _ = tracers.shape
    part = steps * CHUNK * levels
    return pl.CostEstimate(
        flops=part * count * 10, bytes_accessed=part * (count * 8 + 8), transcendentals=0
    )


def payload_kernel(buoyancy, wet, prior, land, clinic, tropic, out, clinic_out, tropic_out, force, wet_in, prior_in, land_in, sems):
    copies = [
        pltpu.make_async_copy(source, target, sems.at[j])
        for j, (source, target) in enumerate(
            (
                (buoyancy, force),
                (wet, wet_in),
                (prior, prior_in),
                (land, land_in),
                (clinic, clinic_out),
                (tropic, tropic_out),
            )
        )
    ]
    for copy in copies:
        copy.start()
    for copy in copies[1:4]:
        copy.wait()
    levels, blocks, cells = force.shape
    rows = cells // LANES
    wet_now = wet_in[...]
    depth = wet_now.astype(F32)
    first = prior_in[...]
    for r in range(rows):
        lanes = slice(r * LANES, (r + 1) * LANES)
        out[1, :, r, :] = depth[:, lanes]
        out[2, :, r, :] = first[:, lanes]
    out[3] = land_in[...].astype(F32)
    copies[0].wait()
    total = jnp.zeros(wet_now.shape, F32)
    for k in range(levels):
        total = total + (k < wet_now).astype(F32) * force[k].astype(F32)
    for r in range(rows):
        out[0, :, r, :] = total[:, r * LANES : (r + 1) * LANES]
    for copy in copies[4:]:
        copy.wait()


def payload_of(buoyancy, wet, prior, land, clinic, tropic):
    blocks, rows, lanes = land.shape
    return pl.pallas_call(
        payload_kernel,
        in_specs=[HBM] * 6,
        out_specs=[VMEM] * 3,
        out_shape=[
            jax.ShapeDtypeStruct((FIELDS, blocks, rows, lanes), F32),
            jax.ShapeDtypeStruct(clinic.shape, clinic.dtype),
            jax.ShapeDtypeStruct(tropic.shape, tropic.dtype),
        ],
        scratch_shapes=[
            pltpu.VMEM(each.shape, each.dtype) for each in (buoyancy, wet, prior, land)
        ]
        + [pltpu.SemaphoreType.DMA((6,))],
        compiler_params=params(16),
    )(*in_hbm(buoyancy, wet, prior, land, clinic, tropic))


def select_kernel(spread, band_rows, *refs):
    parts = refs[: len(spread)]
    clinic, tropic, _, own, to_pair, to_other, band = refs[len(spread) :]
    blocks = own.shape[1]
    band_width = band.shape[1]
    band_row, column = lax.axis_index("by"), lax.axis_index("bx")
    first_slot = band_row * band_width
    for hop, ref in zip(spread, parts):
        holder = (column ^ hop) * blocks
        for s in range(blocks):
            slot = first_slot + holder + s
            at = clinic[slot] - first_slot
            for f in range(FIELDS - 1):
                for h in range(2):
                    band[f, at, h] = ref[f, s, h * HALO : (h + 1) * HALO]
            at = tropic[slot] - first_slot
            for h in range(2):
                band[FIELDS - 1, at, h] = ref[FIELDS - 1, s, h * HALO : (h + 1) * HALO]

    lane = lax.broadcasted_iota(jnp.int32, (HALO, LANES), 1)

    def sides(f, at, half):
        east = lax.rem(at + 1, band_width)
        west = lax.rem(at + band_width - 1, band_width)
        return jnp.where(
            lane < HALO,
            band[f, east, half],
            jnp.where(lane >= LANES - HALO, band[f, west, half], 0.0),
        )

    for i in range(blocks):
        at = tropic[first_slot + column * blocks + i] - first_slot
        for f in range(FIELDS):
            for h in range(2):
                rows = slice(h * HALO, (h + 1) * HALO)
                own[f, i, rows, 0:LANES] = band[f, at, h]
                own[f, i, rows, LANES : 2 * LANES] = sides(f, at, h)

    odd = lax.rem(band_row, 2)
    for out, move in ((to_pair, 1 - 2 * odd), (to_other, 2 * odd - 1)):
        half = (move + 1) // 2
        other = lax.rem(band_row + move + band_rows, band_rows) * band_width
        packed = [None] * FIELDS
        for i in range(blocks):
            at = tropic[other + column * blocks + i] - other
            for f in range(FIELDS):
                out[f, i] = band[f, at, half]
                beside = sides(f, at, half)
                if i:
                    beside = pltpu.roll(beside, 2 * HALO * i, 1)
                packed[f] = beside if i == 0 else packed[f] + beside
        for f in range(FIELDS):
            out[f, blocks] = packed[f]


def select(spread, band_rows, parts, clinic, tropic, band_width, after):
    blocks, rows, lanes = parts[0].shape[1:]
    assert 2 * HALO * blocks <= LANES
    edge = jax.ShapeDtypeStruct((FIELDS, blocks + 1, HALO, lanes), F32)
    return pl.pallas_call(
        functools.partial(select_kernel, spread, band_rows),
        in_specs=[VMEM] * len(parts) + [SMEM] * 2 + [pl.BlockSpec(memory_space=pl.ANY)],
        out_specs=[VMEM] * 3,
        out_shape=[jax.ShapeDtypeStruct((FIELDS, blocks, rows, 2 * lanes), F32), edge, edge],
        scratch_shapes=[pltpu.VMEM((FIELDS, band_width, rows // HALO, HALO, lanes), F32)],
        compiler_params=params(16),
    )(*parts, clinic, tropic, after)


def two_sum(a, b):
    total = a + b
    part = total - a
    return total, (a - (total - part)) + (b - part)


def split(a):
    scaled = a * 4097.0
    high = scaled - (scaled - a)
    return high, a - high


def pair_add(a, b):
    high, low = two_sum(a[0], b[0])
    low = low + (a[1] + b[1])
    total = high + low
    return total, low - (total - high)


def product(a, b):
    return split_product(a, split(a), b, split(b))


def split_product(a, a_parts, b, b_parts):
    value = a * b
    a_high, a_low = a_parts
    b_high, b_low = b_parts
    error = ((a_high * b_high - value) + a_high * b_low + a_low * b_high) + a_low * b_low
    return value, error


def fold(pair, axis, steps):
    for step in steps:
        pair = pair_add(pair, tuple(pltpu.roll(part, step, axis) for part in pair))
    return pair


def lane_sum(pair):
    high, low = pair
    grid = 384.0 * jnp.max(jnp.abs(high), axis=1, keepdims=True)
    lead = (high + grid) - grid
    rest = jnp.sum((high - lead) + low, axis=1, keepdims=True)
    return two_sum(jnp.sum(lead, axis=1, keepdims=True), rest)


def basis_kernel(levels, band_rows, own, from_pair, from_other, _, vectors, guess, sums, images, vector_parts, image_parts):
    blocks, rows = own.shape[1], own.shape[2]
    tall = rows + 2 * HALO
    inner = slice(HALO, HALO + rows)
    lane = lax.broadcasted_iota(jnp.int32, (HALO, LANES), 1)
    beside = (lane < HALO) | (lane >= LANES - HALO)

    band_row = lax.axis_index("by")
    odd = lax.rem(band_row, 2) == 1

    def edge(from_odd, from_even, present, f, i):
        packed = jnp.where(odd, from_odd[f, blocks], from_even[f, blocks])
        if i:
            packed = pltpu.roll(packed, LANES - 2 * HALO * i, 1)
        middle = jnp.where(odd, from_odd[f, i], from_even[f, i])
        both = jnp.concatenate([middle, jnp.where(beside, packed, 0.0)], axis=1)
        return jnp.where(present, both, 0.0)

    def east(v):
        return pltpu.roll(v, 2 * LANES - 1, 1)

    def west(v):
        return pltpu.roll(v, 1, 1)

    def below(v):
        return pltpu.roll(v, tall - 1, 0)

    def above(v):
        return pltpu.roll(v, 1, 0)

    fields = []
    for i in range(blocks):
        forcing, depth, prior, ocean = (
            jnp.concatenate(
                [
                    edge(from_pair, from_other, band_row > 0, f, i),
                    own[f, i],
                    edge(from_other, from_pair, band_row < band_rows - 1, f, i),
                ],
                axis=0,
            )
            for f in range(FIELDS)
        )
        scale = FACE_SCALE / levels
        east_face = scale * jnp.minimum(depth, east(depth)) * ocean * east(ocean)
        south_face = scale * jnp.minimum(depth, below(depth)) * ocean * below(ocean)
        centre = SURFACE * ocean + (1.0 - ocean)
        diagonal = centre + east_face + west(east_face) + south_face + above(south_face)
        inverse = 1.0 / diagonal

        def operate(v, centre=centre, east_face=east_face, south_face=south_face):
            along = east_face * (v - east(v))
            across = south_face * (v - below(v))
            return centre * v + along - west(along) + across - above(across)

        first = ocean * prior
        residual = ocean * forcing - operate(first)
        guess[i] = first[inner, 0:LANES]
        images[ITERS, slice(i * rows, (i + 1) * rows)] = residual[inner, 0:LANES]
        fields.append((operate, inverse, residual * inverse, None))

    for k in range(ITERS):
        for i, (operate, inverse, v, before) in enumerate(fields):
            place = slice(i * rows, (i + 1) * rows)
            image = operate(v)
            vectors[k, place] = v[inner, 0:LANES]
            images[k, place] = image[inner, 0:LANES]
            if k + 1 < ITERS:
                following = image * inverse
                if k == 1:
                    following = v - following
                elif k > 1:
                    following = 2.0 * (v - following) - before
                fields[i] = (operate, inverse, following, v)

    row_id = lax.broadcasted_iota(jnp.int32, (8, LANES), 0)
    lane_id = lax.broadcasted_iota(jnp.int32, (8, LANES), 1)
    for source, parts in ((vectors, vector_parts), (images, image_parts)):
        for a in range(source.shape[0]):
            for r in range(0, blocks * rows, 8):
                parts[0, a, r : r + 8], parts[1, a, r : r + 8] = split(source[a, r : r + 8])
    placed = None
    for begin in range(0, len(ENTRIES), 8):
        packed = (jnp.zeros((8, LANES), F32),) * 2
        for offset, (a, b) in enumerate(ENTRIES[begin : begin + 8]):
            total = error = None
            for r in range(0, blocks * rows, 8):
                at = slice(r, r + 8)
                value, rest = split_product(
                    vectors[a, at],
                    (vector_parts[0, a, at], vector_parts[1, a, at]),
                    images[b, at],
                    (image_parts[0, b, at], image_parts[1, b, at]),
                )
                if total is None:
                    total, error = value, rest
                else:
                    total, extra = two_sum(total, value)
                    error = error + (rest + extra)
            pair = fold((total, error), 0, (4, 2, 1))
            packed = tuple(jnp.where(row_id == offset, new, old) for new, old in zip(pair, packed))
        high, low = lane_sum(packed)
        high = jnp.where(lane_id == row_id + begin, high, 0.0)
        low = jnp.where(lane_id == row_id + (begin + LANES // 2), low, 0.0)
        placed = high + low if placed is None else placed + high + low
    for step in (4, 2, 1):
        placed = placed + pltpu.roll(placed, step, 0)
    sums[...] = jnp.broadcast_to(placed[0:1][None], sums.shape)


def basis(levels, own, from_pair, from_other, after, band_rows, devices):
    fields, blocks, rows, _ = own.shape
    return pl.pallas_call(
        functools.partial(basis_kernel, levels, band_rows),
        in_specs=[VMEM] * 3 + [pl.BlockSpec(memory_space=pl.ANY)],
        out_specs=[VMEM] * 3,
        out_shape=[
            jax.ShapeDtypeStruct((ITERS, blocks * rows, LANES), F32),
            jax.ShapeDtypeStruct((blocks, rows, LANES), F32),
            jax.ShapeDtypeStruct((devices, 1, LANES), F32),
        ],
        scratch_shapes=[
            pltpu.VMEM((ITERS + 1, blocks * rows, LANES), F32),
            pltpu.VMEM((2, ITERS, blocks * rows, LANES), F32),
            pltpu.VMEM((2, ITERS + 1, blocks * rows, LANES), F32),
        ],
        compiler_params=params(16),
    )(own, from_pair, from_other, after)


def finish_kernel(sums, vectors, guess, out):
    devices = sums.shape[0]
    blocks, rows = guess.shape[0], guess.shape[1]
    pairs = [(sums[d : d + 8], jnp.zeros((8, LANES), F32)) for d in range(0, devices, 8)]
    while len(pairs) > 1:
        pairs = [pair_add(pairs[j], pairs[j + 1]) for j in range(0, len(pairs), 2)]
    total, error = fold(pairs[0], 0, (4, 2, 1))
    low = error + pltpu.roll(total, 64, 1)
    entry = {
        pair: tuple(jnp.broadcast_to(part[:, n : n + 1], (8, LANES)) for part in (total, low))
        for n, pair in enumerate(ENTRIES)
    }
    energy = [entry[k, k][0] for k in range(ITERS)]
    inverse, below = [], {}
    for k in range(ITERS):
        pivot = entry[k, k]
        good = pivot[0] > PIVOT_FLOOR * energy[k]
        inverse.append(jnp.where(good, 1.0 / jnp.where(good, pivot[0], 1.0), 0.0))
        for i in range(k + 1, ITERS):
            side = entry[k, i]
            lead = side[0] * inverse[k]
            value, error = product(lead, pivot[0])
            rest = ((side[0] - value) - error) + (side[1] - lead * pivot[1])
            below[i, k] = (lead, rest * inverse[k])
        for i in range(k + 1, ITERS):
            lead, rest = below[i, k]
            for j in range(i, ITERS + 1):
                across = entry[k, j]
                value, error = product(lead, across[0])
                error = error + (lead * across[1] + rest * across[0])
                entry[i, j] = pair_add(entry[i, j], (-value, -error))
    weights = [entry[k, ITERS][0] * inverse[k] for k in range(ITERS)]
    for k in range(ITERS - 2, -1, -1):
        for i in range(ITERS - 1, k, -1):
            weights[k] = weights[k] - below[i, k][0] * weights[i]
    for b in range(blocks):
        for r in range(0, rows, 8):
            at = b * rows + r
            result = guess[b, r : r + 8]
            for k in range(ITERS):
                result = result + weights[k] * vectors[k, at : at + 8]
            out[b, r : r + 8] = result


def finish(sums, vectors, guess):
    return pl.pallas_call(
        finish_kernel,
        in_specs=[VMEM] * 3,
        out_specs=VMEM,
        out_shape=jax.ShapeDtypeStruct(guess.shape, F32),
        compiler_params=params(16),
    )(sums, vectors, guess)


def swap(array, axis, hop):
    count = lax.axis_size(axis)
    return lax.ppermute(array, axis, [(i, i ^ hop) for i in range(count)])


def other_partners(band_rows, holders):
    pairs = []
    for row in range(band_rows):
        other = ((row + 1) ^ 1) - 1
        for column in range(holders):
            inside = 0 <= other < band_rows
            target = (other, column) if inside else (row, column ^ 1)
            pairs.append((row * holders + column, target[0] * holders + target[1]))
    return pairs


def local(
    tracers,
    vertical_speed,
    diffusivity,
    buoyancy_force,
    wet_levels,
    surface_patch,
    prior_height,
    land_mask,
    baroclinic_map,
    barotropic_map,
):
    levels, blocks, _, cells = tracers.shape
    band_rows, holders = lax.axis_size("by"), lax.axis_size("bx")
    early = cells // CHUNK * blocks * EARLY // 16

    payload, clinic, tropic = payload_of(
        buoyancy_force, wet_levels, prior_height, land_mask, baroclinic_map, barotropic_map
    )
    spread = list(range(0, holders, 2))
    parts = [payload] + [swap(payload, "bx", hop) for hop in spread[1:]]
    stepped, mark, regions, *factors = first_columns(
        tracers, vertical_speed, diffusivity, wet_levels, surface_patch, early, payload
    )
    beside = swap(payload, "bx", 1)
    beside, *parts, mark = lax.optimization_barrier((beside, *parts, mark))
    parts = parts + [beside] + [swap(part, "bx", 1) for part in parts[1:]]
    spread = spread + [hop + 1 for hop in spread]

    own, to_pair, to_other = select(
        tuple(spread), band_rows, parts, clinic, tropic, holders * blocks, mark
    )
    from_pair = swap(to_pair, "by", 1)
    from_other = lax.ppermute(to_other, ("by", "bx"), other_partners(band_rows, holders))
    stepped, late = rest_columns(tracers, early, stepped, regions, factors, to_other)
    from_pair, from_other, late = lax.optimization_barrier((from_pair, from_other, late))
    vectors, guess, sums = basis(
        levels, own, from_pair, from_other, late, band_rows, band_rows * holders
    )
    gathered = lax.all_to_all(sums, ("by", "bx"), 0, 0, tiled=True)
    gathered = gathered.reshape(band_rows * holders, LANES)
    return stepped, finish(gathered, vectors, guess)


def solution(mesh):
    slots = ("by", "bx")
    return jax.shard_map(
        local,
        mesh=mesh,
        in_specs=(
            P(None, slots, None, None),
            P(None, slots, None),
            P(None, slots, None),
            P(None, slots, None),
            P(slots, None),
            P(slots, None),
            P(slots, None),
            P(slots, None, None),
            P(),
            P(),
        ),
        out_specs=(P(None, slots, None, None), P(slots, None, None)),
        check_vma=False,
    )
```

```python
import functools

import jax
import jax.numpy as jnp
from jax import lax
from jax.experimental import pallas as pl
from jax.experimental.pallas import tpu as pltpu
from jax.sharding import PartitionSpec as P

ITERS = 6
RESTORE = 0.5
SURFACE = 0.1
FACE_SCALE = 2.0
PIVOT_FLOOR = 1e-11
HALO = 8
LANES = 128
FIELDS = 4
ENTRIES = [(a, b) for a in range(ITERS) for b in range(a, ITERS + 1)]
CHUNK = 512
EARLY = 7
F32 = jnp.float32
VMEM = pl.BlockSpec(memory_space=pltpu.VMEM)
SMEM = pl.BlockSpec(memory_space=pltpu.SMEM)
HBM = pl.BlockSpec(memory_space=pltpu.HBM)


def in_hbm(*arrays):
    return [pltpu.with_memory_space_constraint(array, pltpu.HBM) for array in arrays]


def params(mebibytes):
    return pltpu.CompilerParams(vmem_limit_bytes=mebibytes * 2**20)


def fold_columns(speed, mixing, wet, patch, regions, factors):
    enter, keep, raise_, lower, sink = factors
    levels = speed.shape[0]
    tiles = speed.shape[2] // LANES

    def stacked(block):
        return jnp.concatenate([block[:, t * LANES : (t + 1) * LANES] for t in range(tiles)], axis=0)

    regions[...] = stacked(patch[...])
    wet_now = stacked(wet[...])
    zero = jnp.zeros(wet_now.shape, F32)
    mix_above, up_above, down_above, inverse = zero, zero, zero, zero
    for k in range(levels):
        is_wet = (k < wet_now).astype(F32)
        is_open = (k + 1 < wet_now).astype(F32)
        flow = stacked(speed[k]) * is_open
        up, down = jnp.maximum(flow, 0.0), jnp.minimum(flow, 0.0)
        mix = stacked(mixing[k]) * is_open
        diagonal = 1.0 + mix + mix_above
        if k == 0:
            source = RESTORE * is_wet
            diagonal = diagonal + source
        inverse = 1.0 / (diagonal - mix_above * (mix_above * inverse))
        scaled_wet = is_wet * inverse
        keep[k] = scaled_wet * (1.0 + down - up_above)
        raise_[k] = scaled_wet * up
        lower[k] = mix * inverse
        enter[k] = (source if k == 0 else mix_above) * inverse
        sink[k] = scaled_wet * down_above
        mix_above, up_above, down_above = mix, up, down


def sweep(begin, tracers, out, regions, factors, held, in_sems, out_sems, ready=None):
    enter, keep, raise_, lower, sink = factors
    steps, levels, count, width = held.shape
    blocks = out.shape[1]
    tiles = width // LANES

    def place(ref, j):
        slot = lax.rem(j + begin, blocks)
        at = pl.multiple_of((j + begin) // blocks * width, width)
        return ref.at[:, slot, :, pl.ds(at, width)]

    def load(j):
        return pltpu.make_async_copy(place(tracers, j), held.at[j], in_sems.at[j])

    def store(j):
        return pltpu.make_async_copy(held.at[j], place(out, j), out_sems.at[j])

    tracer_ids = lax.broadcasted_iota(jnp.int32, (count, width), 0)

    def solve(j, carry):
        if ready is None:
            load(j).wait()
        slot = lax.rem(j + begin, blocks)
        first = (j + begin) // blocks * tiles

        def rows(take):
            return jnp.concatenate(
                [
                    jnp.broadcast_to(take(pl.ds((first + t) * blocks + slot, 1)), (count, LANES))
                    for t in range(tiles)
                ],
                axis=1,
            )

        def row(ref, k):
            return rows(lambda at: ref[k, at, :])

        above = value = None
        def given(k):
            if ready is None:
                return held[j, k]
            at = pl.multiple_of((j + begin) // blocks * width, width)
            return ready[k, slot, :, pl.ds(at, width)]

        here = given(0)
        for k in range(levels):
            result = row(keep, k) * here
            if k + 1 < levels:
                below = given(k + 1)
                result = result + row(raise_, k) * below
            if k == 0:
                target = (rows(lambda at: regions[at, :]) == tracer_ids).astype(F32)
                result = result + row(enter, k) * target
            else:
                result = result - row(sink, k) * above
                result = result + row(enter, k) * value
            value = result
            held[j, k] = value
            if k + 1 < levels:
                above, here = here, below
        for k in range(levels - 2, -1, -1):
            value = held[j, k] + row(lower, k) * value
            held[j, k] = value
        store(j).start()
        return carry

    def run(prepare):
        for j in range(steps if ready is None else 0):
            load(j).start()
        prepare()
        lax.fori_loop(0, steps, solve, 0)
        for j in range(steps):
            store(j).wait()

    return run


def first_columns_kernel(tracers, speed, mixing, wet, patch, after, out, mark, regions, *rest):
    factors, (held, speed_in, mixing_in, wet_in, patch_in, sems, in_sems, out_sems) = rest[:5], rest[5:]
    copies = [
        pltpu.make_async_copy(source, target, sems.at[j])
        for j, (source, target) in enumerate(
            ((speed, speed_in), (mixing, mixing_in), (wet, wet_in), (patch, patch_in))
        )
    ]
    for copy in copies:
        copy.start()

    def prepare():
        for copy in copies:
            copy.wait()
        fold_columns(speed_in, mixing_in, wet_in, patch_in, regions, factors)

    mark[...] = jnp.zeros(mark.shape, F32)
    sweep(0, tracers, out, regions, factors, held, in_sems, out_sems)(prepare)


def first_columns(tracers, speed, mixing, wet, patch, steps, after):
    levels, blocks, count, cells = tracers.shape
    rows = cells // LANES * blocks
    factor = jax.ShapeDtypeStruct((levels, rows, LANES), F32)
    return pl.pallas_call(
        first_columns_kernel,
        in_specs=[HBM] * 5 + [pl.BlockSpec(memory_space=pl.ANY)],
        out_specs=[HBM] + [VMEM] * 7,
        out_shape=[
            jax.ShapeDtypeStruct(tracers.shape, F32),
            jax.ShapeDtypeStruct((8, LANES), F32),
            jax.ShapeDtypeStruct((rows, LANES), jnp.int32),
        ]
        + [factor] * 5,
        scratch_shapes=[pltpu.VMEM((steps, levels, count, CHUNK), F32)]
        + [pltpu.VMEM(each.shape, each.dtype) for each in (speed, mixing, wet, patch)]
        + [pltpu.SemaphoreType.DMA((n,)) for n in (4, steps, steps)],
        compiler_params=params(40),
        cost_estimate=column_cost(tracers, steps),
    )(*in_hbm(tracers, speed, mixing, wet, patch), after)


def rest_columns_kernel(begin, tracers, regions, *rest):
    factors, (_, _, out, mark, held, in_sems, out_sems) = rest[:5], rest[5:]
    mark[...] = jnp.zeros(mark.shape, F32)
    sweep(begin, None, out, regions, factors, held, in_sems, out_sems, tracers)(lambda: None)


def rest_columns(tracers, begin, previous, regions, factors, after):
    levels, blocks, count, cells = tracers.shape
    steps = cells // CHUNK * blocks - begin
    return pl.pallas_call(
        functools.partial(rest_columns_kernel, begin),
        in_specs=[VMEM] * 7 + [HBM, pl.BlockSpec(memory_space=pl.ANY)],
        out_specs=[HBM, VMEM],
        out_shape=[
            jax.ShapeDtypeStruct(previous.shape, F32),
            jax.ShapeDtypeStruct((8, LANES), F32),
        ],
        scratch_shapes=[pltpu.VMEM((steps, levels, count, CHUNK), F32)]
        + [pltpu.SemaphoreType.DMA((steps,))] * 2,
        input_output_aliases={7: 0},
        compiler_params=params(24),
        cost_estimate=column_cost(tracers, steps),
    )(tracers, regions, *factors, *in_hbm(previous), after)


def column_cost(tracers, steps):
    levels, _, count, _ = tracers.shape
    part = steps * CHUNK * levels
    return pl.CostEstimate(
        flops=part * count * 10, bytes_accessed=part * (count * 8 + 8), transcendentals=0
    )


def payload_kernel(buoyancy, wet, prior, land, clinic, tropic, out, clinic_out, tropic_out, force, wet_in, prior_in, land_in, sems):
    copies = [
        pltpu.make_async_copy(source, target, sems.at[j])
        for j, (source, target) in enumerate(
            (
                (buoyancy, force),
                (wet, wet_in),
                (prior, prior_in),
                (land, land_in),
                (clinic, clinic_out),
                (tropic, tropic_out),
            )
        )
    ]
    for copy in copies:
        copy.start()
    for copy in copies[1:4]:
        copy.wait()
    levels, blocks, cells = force.shape
    rows = cells // LANES
    wet_now = wet_in[...]
    depth = wet_now.astype(F32)
    first = prior_in[...]
    for r in range(rows):
        lanes = slice(r * LANES, (r + 1) * LANES)
        out[1, :, r, :] = depth[:, lanes]
        out[2, :, r, :] = first[:, lanes]
    out[3] = land_in[...].astype(F32)
    copies[0].wait()
    total = jnp.zeros(wet_now.shape, F32)
    for k in range(levels):
        total = total + (k < wet_now).astype(F32) * force[k].astype(F32)
    for r in range(rows):
        out[0, :, r, :] = total[:, r * LANES : (r + 1) * LANES]
    for copy in copies[4:]:
        copy.wait()


def payload_of(buoyancy, wet, prior, land, clinic, tropic):
    blocks, rows, lanes = land.shape
    return pl.pallas_call(
        payload_kernel,
        in_specs=[HBM] * 6,
        out_specs=[VMEM] * 3,
        out_shape=[
            jax.ShapeDtypeStruct((FIELDS, blocks, rows, lanes), F32),
            jax.ShapeDtypeStruct(clinic.shape, clinic.dtype),
            jax.ShapeDtypeStruct(tropic.shape, tropic.dtype),
        ],
        scratch_shapes=[
            pltpu.VMEM(each.shape, each.dtype) for each in (buoyancy, wet, prior, land)
        ]
        + [pltpu.SemaphoreType.DMA((6,))],
        compiler_params=params(16),
    )(*in_hbm(buoyancy, wet, prior, land, clinic, tropic))


def select_kernel(spread, band_rows, *refs):
    parts = refs[: len(spread)]
    clinic, tropic, _, own, to_pair, to_other, band = refs[len(spread) :]
    blocks = own.shape[1]
    band_width = band.shape[1]
    band_row, column = lax.axis_index("by"), lax.axis_index("bx")
    first_slot = band_row * band_width
    for hop, ref in zip(spread, parts):
        holder = (column ^ hop) * blocks
        for s in range(blocks):
            slot = first_slot + holder + s
            at = clinic[slot] - first_slot
            for f in range(FIELDS - 1):
                for h in range(2):
                    band[f, at, h] = ref[f, s, h * HALO : (h + 1) * HALO]
            at = tropic[slot] - first_slot
            for h in range(2):
                band[FIELDS - 1, at, h] = ref[FIELDS - 1, s, h * HALO : (h + 1) * HALO]

    lane = lax.broadcasted_iota(jnp.int32, (HALO, LANES), 1)

    def sides(f, at, half):
        east = lax.rem(at + 1, band_width)
        west = lax.rem(at + band_width - 1, band_width)
        return jnp.where(
            lane < HALO,
            band[f, east, half],
            jnp.where(lane >= LANES - HALO, band[f, west, half], 0.0),
        )

    for i in range(blocks):
        at = tropic[first_slot + column * blocks + i] - first_slot
        for f in range(FIELDS):
            for h in range(2):
                rows = slice(h * HALO, (h + 1) * HALO)
                own[f, i, rows, 0:LANES] = band[f, at, h]
                own[f, i, rows, LANES : 2 * LANES] = sides(f, at, h)

    odd = lax.rem(band_row, 2)
    for out, move in ((to_pair, 1 - 2 * odd), (to_other, 2 * odd - 1)):
        half = (move + 1) // 2
        other = lax.rem(band_row + move + band_rows, band_rows) * band_width
        packed = [None] * FIELDS
        for i in range(blocks):
            at = tropic[other + column * blocks + i] - other
            for f in range(FIELDS):
                out[f, i] = band[f, at, half]
                beside = sides(f, at, half)
                if i:
                    beside = pltpu.roll(beside, 2 * HALO * i, 1)
                packed[f] = beside if i == 0 else packed[f] + beside
        for f in range(FIELDS):
            out[f, blocks] = packed[f]


def select(spread, band_rows, parts, clinic, tropic, band_width, after):
    blocks, rows, lanes = parts[0].shape[1:]
    assert 2 * HALO * blocks <= LANES
    edge = jax.ShapeDtypeStruct((FIELDS, blocks + 1, HALO, lanes), F32)
    return pl.pallas_call(
        functools.partial(select_kernel, spread, band_rows),
        in_specs=[VMEM] * len(parts) + [SMEM] * 2 + [pl.BlockSpec(memory_space=pl.ANY)],
        out_specs=[VMEM] * 3,
        out_shape=[jax.ShapeDtypeStruct((FIELDS, blocks, rows, 2 * lanes), F32), edge, edge],
        scratch_shapes=[pltpu.VMEM((FIELDS, band_width, rows // HALO, HALO, lanes), F32)],
        compiler_params=params(16),
    )(*parts, clinic, tropic, after)


def two_sum(a, b):
    total = a + b
    part = total - a
    return total, (a - (total - part)) + (b - part)


def split(a):
    scaled = a * 4097.0
    high = scaled - (scaled - a)
    return high, a - high


def pair_add(a, b):
    high, low = two_sum(a[0], b[0])
    low = low + (a[1] + b[1])
    total = high + low
    return total, low - (total - high)


def product(a, b):
    return split_product(a, split(a), b, split(b))


def split_product(a, a_parts, b, b_parts):
    value = a * b
    a_high, a_low = a_parts
    b_high, b_low = b_parts
    error = ((a_high * b_high - value) + a_high * b_low + a_low * b_high) + a_low * b_low
    return value, error


def fold(pair, axis, steps):
    for step in steps:
        pair = pair_add(pair, tuple(pltpu.roll(part, step, axis) for part in pair))
    return pair


def lane_sum(pair):
    high, low = pair
    grid = 384.0 * jnp.max(jnp.abs(high), axis=1, keepdims=True)
    lead = (high + grid) - grid
    rest = jnp.sum((high - lead) + low, axis=1, keepdims=True)
    return two_sum(jnp.sum(lead, axis=1, keepdims=True), rest)


def basis_kernel(levels, band_rows, own, from_pair, from_other, _, vectors, guess, sums, images, vector_parts, image_parts):
    blocks, rows = own.shape[1], own.shape[2]
    tall = rows + 2 * HALO
    inner = slice(HALO, HALO + rows)
    lane = lax.broadcasted_iota(jnp.int32, (HALO, LANES), 1)
    beside = (lane < HALO) | (lane >= LANES - HALO)

    band_row = lax.axis_index("by")
    odd = lax.rem(band_row, 2) == 1

    def edge(from_odd, from_even, present, f, i):
        packed = jnp.where(odd, from_odd[f, blocks], from_even[f, blocks])
        if i:
            packed = pltpu.roll(packed, LANES - 2 * HALO * i, 1)
        middle = jnp.where(odd, from_odd[f, i], from_even[f, i])
        both = jnp.concatenate([middle, jnp.where(beside, packed, 0.0)], axis=1)
        return jnp.where(present, both, 0.0)

    def east(v):
        return pltpu.roll(v, 2 * LANES - 1, 1)

    def west(v):
        return pltpu.roll(v, 1, 1)

    def below(v):
        return pltpu.roll(v, tall - 1, 0)

    def above(v):
        return pltpu.roll(v, 1, 0)

    fields = []
    for i in range(blocks):
        forcing, depth, prior, ocean = (
            jnp.concatenate(
                [
                    edge(from_pair, from_other, band_row > 0, f, i),
                    own[f, i],
                    edge(from_other, from_pair, band_row < band_rows - 1, f, i),
                ],
                axis=0,
            )
            for f in range(FIELDS)
        )
        scale = FACE_SCALE / levels
        east_face = scale * jnp.minimum(depth, east(depth)) * ocean * east(ocean)
        south_face = scale * jnp.minimum(depth, below(depth)) * ocean * below(ocean)
        centre = SURFACE * ocean + (1.0 - ocean)
        diagonal = centre + east_face + west(east_face) + south_face + above(south_face)
        inverse = 1.0 / diagonal

        def operate(v, centre=centre, east_face=east_face, south_face=south_face):
            along = east_face * (v - east(v))
            across = south_face * (v - below(v))
            return centre * v + along - west(along) + across - above(across)

        first = ocean * prior
        residual = ocean * forcing - operate(first)
        guess[i] = first[inner, 0:LANES]
        images[ITERS, slice(i * rows, (i + 1) * rows)] = residual[inner, 0:LANES]
        fields.append((operate, inverse, residual * inverse, None))

    for k in range(ITERS):
        for i, (operate, inverse, v, before) in enumerate(fields):
            place = slice(i * rows, (i + 1) * rows)
            image = operate(v)
            vectors[k, place] = v[inner, 0:LANES]
            images[k, place] = image[inner, 0:LANES]
            if k + 1 < ITERS:
                following = image * inverse
                if k == 1:
                    following = v - following
                elif k > 1:
                    following = 2.0 * (v - following) - before
                fields[i] = (operate, inverse, following, v)

    row_id = lax.broadcasted_iota(jnp.int32, (8, LANES), 0)
    lane_id = lax.broadcasted_iota(jnp.int32, (8, LANES), 1)
    for source, parts in ((vectors, vector_parts), (images, image_parts)):
        for a in range(source.shape[0]):
            for r in range(0, blocks * rows, 8):
                parts[0, a, r : r + 8], parts[1, a, r : r + 8] = split(source[a, r : r + 8])
    placed = None
    for begin in range(0, len(ENTRIES), 8):
        packed = (jnp.zeros((8, LANES), F32),) * 2
        for offset, (a, b) in enumerate(ENTRIES[begin : begin + 8]):
            total = error = None
            for r in range(0, blocks * rows, 8):
                at = slice(r, r + 8)
                value, rest = split_product(
                    vectors[a, at],
                    (vector_parts[0, a, at], vector_parts[1, a, at]),
                    images[b, at],
                    (image_parts[0, b, at], image_parts[1, b, at]),
                )
                if total is None:
                    total, error = value, rest
                else:
                    total, extra = two_sum(total, value)
                    error = error + (rest + extra)
            pair = fold((total, error), 0, (4, 2, 1))
            packed = tuple(jnp.where(row_id == offset, new, old) for new, old in zip(pair, packed))
        high, low = lane_sum(packed)
        high = jnp.where(lane_id == row_id + begin, high, 0.0)
        low = jnp.where(lane_id == row_id + (begin + LANES // 2), low, 0.0)
        placed = high + low if placed is None else placed + high + low
    for step in (4, 2, 1):
        placed = placed + pltpu.roll(placed, step, 0)
    sums[...] = jnp.broadcast_to(placed[0:1][None], sums.shape)


def basis(levels, own, from_pair, from_other, after, band_rows, devices):
    fields, blocks, rows, _ = own.shape
    return pl.pallas_call(
        functools.partial(basis_kernel, levels, band_rows),
        in_specs=[VMEM] * 3 + [pl.BlockSpec(memory_space=pl.ANY)],
        out_specs=[VMEM] * 3,
        out_shape=[
            jax.ShapeDtypeStruct((ITERS, blocks * rows, LANES), F32),
            jax.ShapeDtypeStruct((blocks, rows, LANES), F32),
            jax.ShapeDtypeStruct((devices, 1, LANES), F32),
        ],
        scratch_shapes=[
            pltpu.VMEM((ITERS + 1, blocks * rows, LANES), F32),
            pltpu.VMEM((2, ITERS, blocks * rows, LANES), F32),
            pltpu.VMEM((2, ITERS + 1, blocks * rows, LANES), F32),
        ],
        compiler_params=params(16),
    )(own, from_pair, from_other, after)


def finish_kernel(mine, theirs, vectors, guess, out):
    devices = mine.shape[0]
    blocks, rows = guess.shape[0], guess.shape[1]
    pairs = [
        (rows[d : d + 8], jnp.zeros((8, LANES), F32))
        for rows in (mine, theirs)
        for d in range(0, devices, 8)
    ]
    while len(pairs) > 1:
        pairs = [pair_add(pairs[j], pairs[j + 1]) for j in range(0, len(pairs), 2)]
    total, error = fold(pairs[0], 0, (4, 2, 1))
    low = error + pltpu.roll(total, 64, 1)
    entry = {
        pair: tuple(jnp.broadcast_to(part[:, n : n + 1], (8, LANES)) for part in (total, low))
        for n, pair in enumerate(ENTRIES)
    }
    energy = [entry[k, k][0] for k in range(ITERS)]
    inverse, below = [], {}
    for k in range(ITERS):
        pivot = entry[k, k]
        good = pivot[0] > PIVOT_FLOOR * energy[k]
        inverse.append(jnp.where(good, 1.0 / jnp.where(good, pivot[0], 1.0), 0.0))
        for i in range(k + 1, ITERS):
            side = entry[k, i]
            lead = side[0] * inverse[k]
            value, error = product(lead, pivot[0])
            rest = ((side[0] - value) - error) + (side[1] - lead * pivot[1])
            below[i, k] = (lead, rest * inverse[k])
        for i in range(k + 1, ITERS):
            lead, rest = below[i, k]
            for j in range(i, ITERS + 1):
                across = entry[k, j]
                value, error = product(lead, across[0])
                error = error + (lead * across[1] + rest * across[0])
                entry[i, j] = pair_add(entry[i, j], (-value, -error))
    weights = [entry[k, ITERS][0] * inverse[k] for k in range(ITERS)]
    for k in range(ITERS - 2, -1, -1):
        for i in range(ITERS - 1, k, -1):
            weights[k] = weights[k] - below[i, k][0] * weights[i]
    for b in range(blocks):
        for r in range(0, rows, 8):
            at = b * rows + r
            result = guess[b, r : r + 8]
            for k in range(ITERS):
                result = result + weights[k] * vectors[k, at : at + 8]
            out[b, r : r + 8] = result


def finish(mine, theirs, vectors, guess):
    return pl.pallas_call(
        finish_kernel,
        in_specs=[VMEM] * 4,
        out_specs=VMEM,
        out_shape=jax.ShapeDtypeStruct(guess.shape, F32),
        compiler_params=params(16),
    )(mine, theirs, vectors, guess)


def swap(array, axis, hop):
    count = lax.axis_size(axis)
    return lax.ppermute(array, axis, [(i, i ^ hop) for i in range(count)])


def other_partners(band_rows, holders):
    pairs = []
    for row in range(band_rows):
        other = ((row + 1) ^ 1) - 1
        for column in range(holders):
            inside = 0 <= other < band_rows
            target = (other, column) if inside else (row, column ^ 1)
            pairs.append((row * holders + column, target[0] * holders + target[1]))
    return pairs


def local(
    tracers,
    vertical_speed,
    diffusivity,
    buoyancy_force,
    wet_levels,
    surface_patch,
    prior_height,
    land_mask,
    baroclinic_map,
    barotropic_map,
):
    levels, blocks, _, cells = tracers.shape
    band_rows, holders = lax.axis_size("by"), lax.axis_size("bx")
    early = cells // CHUNK * blocks * EARLY // 16

    payload, clinic, tropic = payload_of(
        buoyancy_force, wet_levels, prior_height, land_mask, baroclinic_map, barotropic_map
    )
    spread = list(range(0, holders, 2))
    parts = [payload] + [swap(payload, "bx", hop) for hop in spread[1:]]
    stepped, mark, regions, *factors = first_columns(
        tracers, vertical_speed, diffusivity, wet_levels, surface_patch, early, payload
    )
    beside = swap(payload, "bx", 1)
    beside, *parts, mark = lax.optimization_barrier((beside, *parts, mark))
    parts = parts + [beside] + [swap(part, "bx", 1) for part in parts[1:]]
    spread = spread + [hop + 1 for hop in spread]

    own, to_pair, to_other = select(
        tuple(spread), band_rows, parts, clinic, tropic, holders * blocks, mark
    )
    from_pair = swap(to_pair, "by", 1)
    from_other = lax.ppermute(to_other, ("by", "bx"), other_partners(band_rows, holders))
    stepped, late = rest_columns(tracers, early, stepped, regions, factors, to_other)
    from_pair, from_other, late = lax.optimization_barrier((from_pair, from_other, late))
    vectors, guess, sums = basis(
        levels, own, from_pair, from_other, late, band_rows, band_rows * holders // 2
    )
    peers = band_rows * holders // 2
    gathered = lax.all_to_all(
        sums,
        ("by", "bx"),
        0,
        0,
        tiled=True,
        axis_index_groups=[list(range(side, 2 * peers, 2))[::-1] for side in range(2)],
    )
    beside = swap(gathered, "bx", 1).reshape(peers, LANES)
    gathered = gathered.reshape(peers, LANES)
    return stepped, finish(gathered, beside, vectors, guess)


def solution(mesh):
    slots = ("by", "bx")
    return jax.shard_map(
        local,
        mesh=mesh,
        in_specs=(
            P(None, slots, None, None),
            P(None, slots, None),
            P(None, slots, None),
            P(None, slots, None),
            P(slots, None),
            P(slots, None),
            P(slots, None),
            P(slots, None, None),
            P(),
            P(),
        ),
        out_specs=(P(None, slots, None, None), P(slots, None, None)),
        check_vma=False,
    )
```

```python
import functools

import jax
import jax.numpy as jnp
from jax import lax
from jax.experimental import pallas as pl
from jax.experimental.pallas import tpu as pltpu
from jax.sharding import PartitionSpec as P

ITERS = 6
RESTORE = 0.5
SURFACE = 0.1
FACE_SCALE = 2.0
PIVOT_FLOOR = 1e-11
HALO = 8
LANES = 128
FIELDS = 4
ENTRIES = [(a, b) for a in range(ITERS) for b in range(a, ITERS + 1)]
CHUNK = 512
EARLY = 5
F32 = jnp.float32
VMEM = pl.BlockSpec(memory_space=pltpu.VMEM)
SMEM = pl.BlockSpec(memory_space=pltpu.SMEM)
HBM = pl.BlockSpec(memory_space=pltpu.HBM)


def in_hbm(*arrays):
    return [pltpu.with_memory_space_constraint(array, pltpu.HBM) for array in arrays]


def params(mebibytes):
    return pltpu.CompilerParams(vmem_limit_bytes=mebibytes * 2**20)


def fold_columns(speed, mixing, wet, patch, regions, factors):
    enter, keep, raise_, lower, sink = factors
    levels = speed.shape[0]
    tiles = speed.shape[2] // LANES

    def stacked(block):
        return jnp.concatenate([block[:, t * LANES : (t + 1) * LANES] for t in range(tiles)], axis=0)

    regions[...] = stacked(patch[...])
    wet_now = stacked(wet[...])
    zero = jnp.zeros(wet_now.shape, F32)
    mix_above, up_above, down_above, inverse = zero, zero, zero, zero
    for k in range(levels):
        is_wet = (k < wet_now).astype(F32)
        is_open = (k + 1 < wet_now).astype(F32)
        flow = stacked(speed[k]) * is_open
        up, down = jnp.maximum(flow, 0.0), jnp.minimum(flow, 0.0)
        mix = stacked(mixing[k]) * is_open
        diagonal = 1.0 + mix + mix_above
        if k == 0:
            source = RESTORE * is_wet
            diagonal = diagonal + source
        inverse = 1.0 / (diagonal - mix_above * (mix_above * inverse))
        scaled_wet = is_wet * inverse
        keep[k] = scaled_wet * (1.0 + down - up_above)
        raise_[k] = scaled_wet * up
        lower[k] = mix * inverse
        enter[k] = (source if k == 0 else mix_above) * inverse
        sink[k] = scaled_wet * down_above
        mix_above, up_above, down_above = mix, up, down


def sweep(begin, tracers, out, regions, factors, held, in_sems, out_sems, ready=None):
    enter, keep, raise_, lower, sink = factors
    steps, levels, count, width = held.shape
    blocks = out.shape[1]
    tiles = width // LANES

    def place(ref, j):
        slot = lax.rem(j + begin, blocks)
        at = pl.multiple_of((j + begin) // blocks * width, width)
        return ref.at[:, slot, :, pl.ds(at, width)]

    def load(j):
        return pltpu.make_async_copy(place(tracers, j), held.at[j], in_sems.at[j])

    def store(j):
        return pltpu.make_async_copy(held.at[j], place(out, j), out_sems.at[j])

    tracer_ids = lax.broadcasted_iota(jnp.int32, (count, width), 0)

    def solve(j, carry):
        if ready is None:
            load(j).wait()
        slot = lax.rem(j + begin, blocks)
        first = (j + begin) // blocks * tiles

        def rows(take):
            return jnp.concatenate(
                [
                    jnp.broadcast_to(take(pl.ds((first + t) * blocks + slot, 1)), (count, LANES))
                    for t in range(tiles)
                ],
                axis=1,
            )

        def row(ref, k):
            return rows(lambda at: ref[k, at, :])

        above = value = None
        def given(k):
            if ready is None:
                return held[j, k]
            at = pl.multiple_of((j + begin) // blocks * width, width)
            return ready[k, slot, :, pl.ds(at, width)]

        here = given(0)
        for k in range(levels):
            result = row(keep, k) * here
            if k + 1 < levels:
                below = given(k + 1)
                result = result + row(raise_, k) * below
            if k == 0:
                target = (rows(lambda at: regions[at, :]) == tracer_ids).astype(F32)
                result = result + row(enter, k) * target
            else:
                result = result - row(sink, k) * above
                result = result + row(enter, k) * value
            value = result
            held[j, k] = value
            if k + 1 < levels:
                above, here = here, below
        for k in range(levels - 2, -1, -1):
            value = held[j, k] + row(lower, k) * value
            held[j, k] = value
        store(j).start()
        return carry

    def run(prepare):
        for j in range(steps if ready is None else 0):
            load(j).start()
        prepare()
        lax.fori_loop(0, steps, solve, 0)
        for j in range(steps):
            store(j).wait()

    return run


def first_columns_kernel(tracers, speed, mixing, wet, patch, after, out, mark, regions, *rest):
    factors, (held, speed_in, mixing_in, wet_in, patch_in, sems, in_sems, out_sems) = rest[:5], rest[5:]
    copies = [
        pltpu.make_async_copy(source, target, sems.at[j])
        for j, (source, target) in enumerate(
            ((speed, speed_in), (mixing, mixing_in), (wet, wet_in), (patch, patch_in))
        )
    ]
    for copy in copies:
        copy.start()

    def prepare():
        for copy in copies:
            copy.wait()
        fold_columns(speed_in, mixing_in, wet_in, patch_in, regions, factors)

    mark[...] = jnp.zeros(mark.shape, F32)
    sweep(0, tracers, out, regions, factors, held, in_sems, out_sems)(prepare)


def first_columns(tracers, speed, mixing, wet, patch, steps, after):
    levels, blocks, count, cells = tracers.shape
    rows = cells // LANES * blocks
    factor = jax.ShapeDtypeStruct((levels, rows, LANES), F32)
    return pl.pallas_call(
        first_columns_kernel,
        in_specs=[HBM] * 5 + [pl.BlockSpec(memory_space=pl.ANY)],
        out_specs=[HBM] + [VMEM] * 7,
        out_shape=[
            jax.ShapeDtypeStruct(tracers.shape, F32),
            jax.ShapeDtypeStruct((8, LANES), F32),
            jax.ShapeDtypeStruct((rows, LANES), jnp.int32),
        ]
        + [factor] * 5,
        scratch_shapes=[pltpu.VMEM((steps, levels, count, CHUNK), F32)]
        + [pltpu.VMEM(each.shape, each.dtype) for each in (speed, mixing, wet, patch)]
        + [pltpu.SemaphoreType.DMA((n,)) for n in (4, steps, steps)],
        compiler_params=params(40),
        cost_estimate=column_cost(tracers, steps),
    )(*in_hbm(tracers, speed, mixing, wet, patch), after)


def rest_columns_kernel(begin, tracers, regions, *rest):
    factors, (_, _, out, mark, held, in_sems, out_sems) = rest[:5], rest[5:]
    mark[...] = jnp.zeros(mark.shape, F32)
    sweep(begin, None, out, regions, factors, held, in_sems, out_sems, tracers)(lambda: None)


def rest_columns(tracers, begin, previous, regions, factors, after):
    levels, blocks, count, cells = tracers.shape
    steps = cells // CHUNK * blocks - begin
    return pl.pallas_call(
        functools.partial(rest_columns_kernel, begin),
        in_specs=[VMEM] * 7 + [HBM, pl.BlockSpec(memory_space=pl.ANY)],
        out_specs=[HBM, VMEM],
        out_shape=[
            jax.ShapeDtypeStruct(previous.shape, F32),
            jax.ShapeDtypeStruct((8, LANES), F32),
        ],
        scratch_shapes=[pltpu.VMEM((steps, levels, count, CHUNK), F32)]
        + [pltpu.SemaphoreType.DMA((steps,))] * 2,
        input_output_aliases={7: 0},
        compiler_params=params(24),
        cost_estimate=column_cost(tracers, steps),
    )(tracers, regions, *factors, *in_hbm(previous), after)


def column_cost(tracers, steps):
    levels, _, count, _ = tracers.shape
    part = steps * CHUNK * levels
    return pl.CostEstimate(
        flops=part * count * 10, bytes_accessed=part * (count * 8 + 8), transcendentals=0
    )


def payload_kernel(buoyancy, wet, prior, land, clinic, tropic, out, clinic_out, tropic_out, force, wet_in, prior_in, land_in, sems):
    copies = [
        pltpu.make_async_copy(source, target, sems.at[j])
        for j, (source, target) in enumerate(
            (
                (buoyancy, force),
                (wet, wet_in),
                (prior, prior_in),
                (land, land_in),
                (clinic, clinic_out),
                (tropic, tropic_out),
            )
        )
    ]
    for copy in copies:
        copy.start()
    for copy in copies[1:4]:
        copy.wait()
    levels, blocks, cells = force.shape
    rows = cells // LANES
    wet_now = wet_in[...]
    depth = wet_now.astype(F32)
    first = prior_in[...]
    for r in range(rows):
        lanes = slice(r * LANES, (r + 1) * LANES)
        out[1, :, r, :] = depth[:, lanes]
        out[2, :, r, :] = first[:, lanes]
    out[3] = land_in[...].astype(F32)
    copies[0].wait()
    total = jnp.zeros(wet_now.shape, F32)
    for k in range(levels):
        total = total + (k < wet_now).astype(F32) * force[k].astype(F32)
    for r in range(rows):
        out[0, :, r, :] = total[:, r * LANES : (r + 1) * LANES]
    for copy in copies[4:]:
        copy.wait()


def payload_of(buoyancy, wet, prior, land, clinic, tropic):
    blocks, rows, lanes = land.shape
    return pl.pallas_call(
        payload_kernel,
        in_specs=[HBM] * 6,
        out_specs=[VMEM] * 3,
        out_shape=[
            jax.ShapeDtypeStruct((FIELDS, blocks, rows, lanes), F32),
            jax.ShapeDtypeStruct(clinic.shape, clinic.dtype),
            jax.ShapeDtypeStruct(tropic.shape, tropic.dtype),
        ],
        scratch_shapes=[
            pltpu.VMEM(each.shape, each.dtype) for each in (buoyancy, wet, prior, land)
        ]
        + [pltpu.SemaphoreType.DMA((6,))],
        compiler_params=params(16),
    )(*in_hbm(buoyancy, wet, prior, land, clinic, tropic))


def select_kernel(spread, band_rows, *refs):
    parts = refs[: len(spread)]
    clinic, tropic, _, own, to_pair, to_other, band = refs[len(spread) :]
    blocks = own.shape[1]
    band_width = band.shape[1]
    band_row, column = lax.axis_index("by"), lax.axis_index("bx")
    first_slot = band_row * band_width
    for hop, ref in zip(spread, parts):
        holder = (column ^ hop) * blocks
        for s in range(blocks):
            slot = first_slot + holder + s
            at = clinic[slot] - first_slot
            for f in range(FIELDS - 1):
                for h in range(2):
                    band[f, at, h] = ref[f, s, h * HALO : (h + 1) * HALO]
            at = tropic[slot] - first_slot
            for h in range(2):
                band[FIELDS - 1, at, h] = ref[FIELDS - 1, s, h * HALO : (h + 1) * HALO]

    lane = lax.broadcasted_iota(jnp.int32, (HALO, LANES), 1)

    def sides(f, at, half):
        east = lax.rem(at + 1, band_width)
        west = lax.rem(at + band_width - 1, band_width)
        return jnp.where(
            lane < HALO,
            band[f, east, half],
            jnp.where(lane >= LANES - HALO, band[f, west, half], 0.0),
        )

    for i in range(blocks):
        at = tropic[first_slot + column * blocks + i] - first_slot
        for f in range(FIELDS):
            for h in range(2):
                rows = slice(h * HALO, (h + 1) * HALO)
                own[f, i, rows, 0:LANES] = band[f, at, h]
                own[f, i, rows, LANES : 2 * LANES] = sides(f, at, h)

    odd = lax.rem(band_row, 2)
    for out, move in ((to_pair, 1 - 2 * odd), (to_other, 2 * odd - 1)):
        half = (move + 1) // 2
        other = lax.rem(band_row + move + band_rows, band_rows) * band_width
        packed = [None] * FIELDS
        for i in range(blocks):
            at = tropic[other + column * blocks + i] - other
            for f in range(FIELDS):
                out[f, i] = band[f, at, half]
                beside = sides(f, at, half)
                if i:
                    beside = pltpu.roll(beside, 2 * HALO * i, 1)
                packed[f] = beside if i == 0 else packed[f] + beside
        for f in range(FIELDS):
            out[f, blocks] = packed[f]


def select(spread, band_rows, parts, clinic, tropic, band_width, after):
    blocks, rows, lanes = parts[0].shape[1:]
    assert 2 * HALO * blocks <= LANES
    edge = jax.ShapeDtypeStruct((FIELDS, blocks + 1, HALO, lanes), F32)
    return pl.pallas_call(
        functools.partial(select_kernel, spread, band_rows),
        in_specs=[VMEM] * len(parts) + [SMEM] * 2 + [pl.BlockSpec(memory_space=pl.ANY)],
        out_specs=[VMEM] * 3,
        out_shape=[jax.ShapeDtypeStruct((FIELDS, blocks, rows, 2 * lanes), F32), edge, edge],
        scratch_shapes=[pltpu.VMEM((FIELDS, band_width, rows // HALO, HALO, lanes), F32)],
        compiler_params=params(16),
    )(*parts, clinic, tropic, after)


def two_sum(a, b):
    total = a + b
    part = total - a
    return total, (a - (total - part)) + (b - part)


def split(a):
    scaled = a * 4097.0
    high = scaled - (scaled - a)
    return high, a - high


def pair_add(a, b):
    high, low = two_sum(a[0], b[0])
    low = low + (a[1] + b[1])
    total = high + low
    return total, low - (total - high)


def product(a, b):
    return split_product(a, split(a), b, split(b))


def split_product(a, a_parts, b, b_parts):
    value = a * b
    a_high, a_low = a_parts
    b_high, b_low = b_parts
    error = ((a_high * b_high - value) + a_high * b_low + a_low * b_high) + a_low * b_low
    return value, error


def fold(pair, axis, steps):
    for step in steps:
        pair = pair_add(pair, tuple(pltpu.roll(part, step, axis) for part in pair))
    return pair


def lane_sum(pair):
    high, low = pair
    grid = 384.0 * jnp.max(jnp.abs(high), axis=1, keepdims=True)
    lead = (high + grid) - grid
    rest = jnp.sum((high - lead) + low, axis=1, keepdims=True)
    return two_sum(jnp.sum(lead, axis=1, keepdims=True), rest)


def basis_kernel(levels, band_rows, own, from_pair, from_other, _, vectors, guess, sums, images, vector_parts, image_parts):
    blocks, rows = own.shape[1], own.shape[2]
    tall = rows + 2 * HALO
    inner = slice(HALO, HALO + rows)
    lane = lax.broadcasted_iota(jnp.int32, (HALO, LANES), 1)
    beside = (lane < HALO) | (lane >= LANES - HALO)

    band_row = lax.axis_index("by")
    odd = lax.rem(band_row, 2) == 1

    def edge(from_odd, from_even, present, f, i):
        packed = jnp.where(odd, from_odd[f, blocks], from_even[f, blocks])
        if i:
            packed = pltpu.roll(packed, LANES - 2 * HALO * i, 1)
        middle = jnp.where(odd, from_odd[f, i], from_even[f, i])
        both = jnp.concatenate([middle, jnp.where(beside, packed, 0.0)], axis=1)
        return jnp.where(present, both, 0.0)

    def east(v):
        return pltpu.roll(v, 2 * LANES - 1, 1)

    def west(v):
        return pltpu.roll(v, 1, 1)

    def below(v):
        return pltpu.roll(v, tall - 1, 0)

    def above(v):
        return pltpu.roll(v, 1, 0)

    fields = []
    for i in range(blocks):
        forcing, depth, prior, ocean = (
            jnp.concatenate(
                [
                    edge(from_pair, from_other, band_row > 0, f, i),
                    own[f, i],
                    edge(from_other, from_pair, band_row < band_rows - 1, f, i),
                ],
                axis=0,
            )
            for f in range(FIELDS)
        )
        scale = FACE_SCALE / levels
        east_face = scale * jnp.minimum(depth, east(depth)) * ocean * east(ocean)
        south_face = scale * jnp.minimum(depth, below(depth)) * ocean * below(ocean)
        centre = SURFACE * ocean + (1.0 - ocean)
        diagonal = centre + east_face + west(east_face) + south_face + above(south_face)
        inverse = 1.0 / diagonal

        def operate(v, centre=centre, east_face=east_face, south_face=south_face):
            along = east_face * (v - east(v))
            across = south_face * (v - below(v))
            return centre * v + along - west(along) + across - above(across)

        first = ocean * prior
        residual = ocean * forcing - operate(first)
        guess[i] = first[inner, 0:LANES]
        images[ITERS, slice(i * rows, (i + 1) * rows)] = residual[inner, 0:LANES]
        fields.append((operate, inverse, residual * inverse, None))

    for k in range(ITERS):
        for i, (operate, inverse, v, before) in enumerate(fields):
            place = slice(i * rows, (i + 1) * rows)
            image = operate(v)
            vectors[k, place] = v[inner, 0:LANES]
            images[k, place] = image[inner, 0:LANES]
            if k + 1 < ITERS:
                following = image * inverse
                if k == 1:
                    following = v - following
                elif k > 1:
                    following = 2.0 * (v - following) - before
                fields[i] = (operate, inverse, following, v)

    row_id = lax.broadcasted_iota(jnp.int32, (8, LANES), 0)
    lane_id = lax.broadcasted_iota(jnp.int32, (8, LANES), 1)
    for source, parts in ((vectors, vector_parts), (images, image_parts)):
        for a in range(source.shape[0]):
            for r in range(0, blocks * rows, 8):
                parts[0, a, r : r + 8], parts[1, a, r : r + 8] = split(source[a, r : r + 8])
    placed = None
    for begin in range(0, len(ENTRIES), 8):
        packed = (jnp.zeros((8, LANES), F32),) * 2
        for offset, (a, b) in enumerate(ENTRIES[begin : begin + 8]):
            total = error = None
            for r in range(0, blocks * rows, 8):
                at = slice(r, r + 8)
                value, rest = split_product(
                    vectors[a, at],
                    (vector_parts[0, a, at], vector_parts[1, a, at]),
                    images[b, at],
                    (image_parts[0, b, at], image_parts[1, b, at]),
                )
                if total is None:
                    total, error = value, rest
                else:
                    total, extra = two_sum(total, value)
                    error = error + (rest + extra)
            pair = fold((total, error), 0, (4, 2, 1))
            packed = tuple(jnp.where(row_id == offset, new, old) for new, old in zip(pair, packed))
        high, low = lane_sum(packed)
        high = jnp.where(lane_id == row_id + begin, high, 0.0)
        low = jnp.where(lane_id == row_id + (begin + LANES // 2), low, 0.0)
        placed = high + low if placed is None else placed + high + low
    for step in (4, 2, 1):
        placed = placed + pltpu.roll(placed, step, 0)
    sums[...] = jnp.broadcast_to(placed[0:1][None], sums.shape)


def basis(levels, own, from_pair, from_other, after, band_rows, devices):
    fields, blocks, rows, _ = own.shape
    return pl.pallas_call(
        functools.partial(basis_kernel, levels, band_rows),
        in_specs=[VMEM] * 3 + [pl.BlockSpec(memory_space=pl.ANY)],
        out_specs=[VMEM] * 3,
        out_shape=[
            jax.ShapeDtypeStruct((ITERS, blocks * rows, LANES), F32),
            jax.ShapeDtypeStruct((blocks, rows, LANES), F32),
            jax.ShapeDtypeStruct((devices, 1, LANES), F32),
        ],
        scratch_shapes=[
            pltpu.VMEM((ITERS + 1, blocks * rows, LANES), F32),
            pltpu.VMEM((2, ITERS, blocks * rows, LANES), F32),
            pltpu.VMEM((2, ITERS + 1, blocks * rows, LANES), F32),
        ],
        compiler_params=params(16),
    )(own, from_pair, from_other, after)


def finish_kernel(mine, theirs, vectors, guess, out):
    devices = mine.shape[0]
    blocks, rows = guess.shape[0], guess.shape[1]
    pairs = [
        (rows[d : d + 8], jnp.zeros((8, LANES), F32))
        for rows in (mine, theirs)
        for d in range(0, devices, 8)
    ]
    while len(pairs) > 1:
        pairs = [pair_add(pairs[j], pairs[j + 1]) for j in range(0, len(pairs), 2)]
    total, error = fold(pairs[0], 0, (4, 2, 1))
    low = error + pltpu.roll(total, 64, 1)
    entry = {
        pair: tuple(jnp.broadcast_to(part[:, n : n + 1], (8, LANES)) for part in (total, low))
        for n, pair in enumerate(ENTRIES)
    }
    energy = [entry[k, k][0] for k in range(ITERS)]
    inverse, below = [], {}
    for k in range(ITERS):
        pivot = entry[k, k]
        good = pivot[0] > PIVOT_FLOOR * energy[k]
        inverse.append(jnp.where(good, 1.0 / jnp.where(good, pivot[0], 1.0), 0.0))
        for i in range(k + 1, ITERS):
            side = entry[k, i]
            lead = side[0] * inverse[k]
            value, error = product(lead, pivot[0])
            rest = ((side[0] - value) - error) + (side[1] - lead * pivot[1])
            below[i, k] = (lead, rest * inverse[k])
        for i in range(k + 1, ITERS):
            lead, rest = below[i, k]
            for j in range(i, ITERS + 1):
                across = entry[k, j]
                value, error = product(lead, across[0])
                error = error + (lead * across[1] + rest * across[0])
                entry[i, j] = pair_add(entry[i, j], (-value, -error))
    weights = [entry[k, ITERS][0] * inverse[k] for k in range(ITERS)]
    for k in range(ITERS - 2, -1, -1):
        for i in range(ITERS - 1, k, -1):
            weights[k] = weights[k] - below[i, k][0] * weights[i]
    for b in range(blocks):
        for r in range(0, rows, 8):
            at = b * rows + r
            result = guess[b, r : r + 8]
            for k in range(ITERS):
                result = result + weights[k] * vectors[k, at : at + 8]
            out[b, r : r + 8] = result


def finish(mine, theirs, vectors, guess):
    return pl.pallas_call(
        finish_kernel,
        in_specs=[VMEM] * 4,
        out_specs=VMEM,
        out_shape=jax.ShapeDtypeStruct(guess.shape, F32),
        compiler_params=params(16),
    )(mine, theirs, vectors, guess)


def swap(array, axis, hop):
    count = lax.axis_size(axis)
    return lax.ppermute(array, axis, [(i, i ^ hop) for i in range(count)])


def other_partners(band_rows, holders):
    pairs = []
    for row in range(band_rows):
        other = ((row + 1) ^ 1) - 1
        for column in range(holders):
            inside = 0 <= other < band_rows
            target = (other, column) if inside else (row, column ^ 1)
            pairs.append((row * holders + column, target[0] * holders + target[1]))
    return pairs


def local(
    tracers,
    vertical_speed,
    diffusivity,
    buoyancy_force,
    wet_levels,
    surface_patch,
    prior_height,
    land_mask,
    baroclinic_map,
    barotropic_map,
):
    levels, blocks, _, cells = tracers.shape
    band_rows, holders = lax.axis_size("by"), lax.axis_size("bx")
    early = cells // CHUNK * blocks * EARLY // 16

    payload, clinic, tropic = payload_of(
        buoyancy_force, wet_levels, prior_height, land_mask, baroclinic_map, barotropic_map
    )
    spread = list(range(0, holders, 2))
    parts = [payload] + [swap(payload, "bx", hop) for hop in spread[1:]]
    stepped, mark, regions, *factors = first_columns(
        tracers, vertical_speed, diffusivity, wet_levels, surface_patch, early, payload
    )
    beside = swap(payload, "bx", 1)
    beside, *parts[2:], mark = lax.optimization_barrier((beside, *parts[2:], mark))
    parts = parts + [beside] + [swap(part, "bx", 1) for part in parts[1:]]
    spread = spread + [hop + 1 for hop in spread]

    own, to_pair, to_other = select(
        tuple(spread), band_rows, parts, clinic, tropic, holders * blocks, mark
    )
    from_pair = swap(to_pair, "by", 1)
    from_other = lax.ppermute(to_other, ("by", "bx"), other_partners(band_rows, holders))
    stepped, late = rest_columns(tracers, early, stepped, regions, factors, to_other)
    from_pair, from_other, late = lax.optimization_barrier((from_pair, from_other, late))
    vectors, guess, sums = basis(
        levels, own, from_pair, from_other, late, band_rows, band_rows * holders // 2
    )
    peers = band_rows * holders // 2
    gathered = lax.all_to_all(
        sums,
        ("by", "bx"),
        0,
        0,
        tiled=True,
        axis_index_groups=[[(d ^ 22) for d in range(side, 2 * peers, 2)] for side in range(2)],
    )
    beside = swap(gathered, "bx", 1).reshape(peers, LANES)
    gathered = gathered.reshape(peers, LANES)
    return stepped, finish(gathered, beside, vectors, guess)


def solution(mesh):
    slots = ("by", "bx")
    return jax.shard_map(
        local,
        mesh=mesh,
        in_specs=(
            P(None, slots, None, None),
            P(None, slots, None),
            P(None, slots, None),
            P(None, slots, None),
            P(slots, None),
            P(slots, None),
            P(slots, None),
            P(slots, None, None),
            P(),
            P(),
        ),
        out_specs=(P(None, slots, None, None), P(slots, None, None)),
        check_vma=False,
    )
```
